128 devices in a mesh: head: 2 (over y_hi), inner: 4 (over x), outer: 16 (over y_lo, z, core).
Axes of the slice: x: 4, y: 4 (y_hi: 2, y_lo: 2; y = y_hi * 2 + y_lo), z: 4, core: 2. Of those that a mesh axis runs over, the one named last changes fastest.
Arguments:
- queries: bfloat16 [16384, 3072], P(('inner', 'outer'), 'head'), may hold values from -8 to 8
- key_vectors: bfloat16 [16384, 512], P(('inner', 'outer'), 'head'), may hold values from -8 to 8
- value_vectors: bfloat16 [16384, 512], P(('inner', 'outer'), 'head'), may hold values from -6 to 6
- query_taps: float32 [4, 3072], P(None, 'head'), may hold values from 0.1 to 0.6
- key_taps: float32 [4, 512], P(None, 'head'), may hold values from 0.1 to 0.6
- out_weight: bfloat16 [3072, 6144], P('head'), may hold values from -0.109375 to 0.109375
- doc_blocks: int32 [8], replicated, may hold values from 1 to 80, 128 in all
Outputs:
- layer_out: bfloat16 [16384, 6144], P(('inner', 'outer'), 'head')
The draws below stay inside these ranges and needn't reach their ends.
All inputs are finite; a program needn't handle non-finite values.
Results may differ from the reference program's by a relative error of at most 0.013.
Values may be sent and summed in bfloat16 or wider, within the bound.
A program may use at most 128 MiB of HBM per device.

```python
import math
import jax
import jax.numpy as jnp
import numpy as np
from jax import lax

D = 6144
QHEADS = 24
KVHEADS = 4
HD = 128
BLOCK = 128
NDOCS = 8
SEQ = 16384
GROUP = 6
DOC_MOST = 80


def draw_queries(key, part):
    key = jax.random.fold_in(key, 1)
    key_a = jax.random.fold_in(key, 0)
    cols = QHEADS * HD
    values_out = jnp.clip(2.0 * jax.random.normal(key_a, (SEQ, cols), jnp.float32), -8.0, 8.0)
    return values_out.astype(jnp.bfloat16)


def draw_key_vectors(key, part):
    key = jax.random.fold_in(key, 2)
    key_a = jax.random.fold_in(key, 0)
    cols = KVHEADS * HD
    values_out = jnp.clip(2.0 * jax.random.normal(key_a, (SEQ, cols), jnp.float32), -8.0, 8.0)
    return values_out.astype(jnp.bfloat16)


def shard_levels(stream_key, extent, cuts, smallest, largest):
    def one(axis_at, parts):
        draws = jax.random.uniform(jax.random.fold_in(jax.random.fold_in(stream_key, 6), axis_at), (parts,), jnp.float32, smallest / len(cuts), largest / len(cuts))
        return jnp.repeat(jnp.exp(draws), extent[axis_at] // parts).reshape((-1,) + (1,) * (len(extent) - axis_at - 1))

    loudness = one(*cuts[0])
    for cut in cuts[1:]:
        loudness = loudness * one(*cut)
    return loudness


def split_up(amount, total, bound, lean):
    loads = [(1 << 20) // math.isqrt(rank ** lean) + 1 for rank in range(2, amount + 1)]
    rest, given = total - bound - (amount - 1), [1] * (amount - 1)
    while rest > 0:
        candidates = [i for i in range(amount - 1) if given[i] < bound]
        pool, budget = sum([loads[i] for i in candidates]), rest
        for i in candidates:
            extra = min(bound - given[i], max(1, budget * loads[i] // pool), rest)
            given[i] = given[i] + extra
            rest = rest - extra
    return np.array([bound] + given)


def uneven(own_key, number_of, total, most, slope):
    if number_of == 2:
        one = jax.random.randint(own_key, (), max(1, total - most), min(most, total - 1) + 1)
        return jnp.stack([one, total - one])
    lengths = jnp.asarray(split_up(number_of, total, most, slope), jnp.int32)
    couples = (number_of - 1) // 2
    source_of, taker = lengths[1:1 + 2 * couples:2], lengths[2:2 + 2 * couples:2]
    slack = jnp.minimum(source_of - 1, most - taker)
    shifted = jax.random.randint(jax.random.fold_in(own_key, 1), (couples,), 0, 1 << 20) % (slack + 1)
    lengths = lengths.at[1:1 + 2 * couples:2].set(source_of - shifted).at[2:2 + 2 * couples:2].set(taker + shifted)
    return lengths[jax.random.permutation(jax.random.fold_in(own_key, 2), number_of)]


def gaussian(key, shape, scale, limit, cuts=(), kind=jnp.bfloat16):
    loudness = shard_levels(key, shape, cuts, -0.22, 0.18) if cuts else 1.0
    values = jax.random.normal(key, shape, jnp.float32) * scale * loudness
    return jnp.minimum(jnp.maximum(values, -limit), limit).astype(kind)


def setup_inputs(seed: int = 0) -> dict:
    seeds = jax.random.split(jax.random.key(seed), 8)
    return {
        "queries": draw_queries(jax.random.fold_in(seeds[7], 71), 0),
        "key_vectors": draw_key_vectors(jax.random.fold_in(seeds[7], 71), 0),
        "value_vectors": gaussian(seeds[2], (SEQ, KVHEADS * HD), 1.0, 6.0, ((0, 64), (1, 2))),
        "query_taps": jnp.clip(0.1 + 0.5 * jax.random.uniform(seeds[3], (4, QHEADS * HD), jnp.float32) ** shard_levels(seeds[3], (4, QHEADS * HD), ((1, 2),), -0.2, 0.2), 0.1, 0.6),
        "key_taps": jnp.clip(0.1 + 0.5 * jax.random.uniform(seeds[4], (4, KVHEADS * HD), jnp.float32) ** shard_levels(seeds[4], (4, KVHEADS * HD), ((1, 2),), -0.2, 0.2), 0.1, 0.6),
        "out_weight": gaussian(seeds[5], (QHEADS * HD, D), (QHEADS * HD) ** -0.5, 0.109375, ((0, 2),)),
        "doc_blocks": uneven(seeds[6], NDOCS, SEQ // BLOCK, DOC_MOST, 2).astype(jnp.int32),
    }


query_rows = 512


def causal_conv(field, taps):
    wide = field.astype(jnp.float32)
    padded = jnp.concatenate([jnp.zeros((3, wide.shape[1]), jnp.float32), wide], axis=0)
    total = jnp.zeros_like(wide)
    for j in range(4):
        total = total + taps[j][None, :] * padded[3 - j:3 - j + SEQ]
    return total.astype(jnp.bfloat16)


def reference(queries, key_vectors, value_vectors, query_taps, key_taps, out_weight, doc_blocks):
    conv_q = causal_conv(queries, query_taps)
    conv_k = causal_conv(key_vectors, key_taps)
    starts = (jnp.cumsum(doc_blocks) - doc_blocks) * BLOCK
    position = jnp.arange(SEQ, dtype=jnp.int32)
    document = jnp.sum((position[:, None] >= starts[None, :]).astype(jnp.int32), axis=1) - 1
    q_heads = conv_q.reshape(SEQ, KVHEADS, GROUP, HD)
    k_heads = conv_k.reshape(SEQ, KVHEADS, HD)
    v_heads = value_vectors.reshape(SEQ, KVHEADS, HD)
    factor = HD ** -0.5

    def per_block(b):
        first = (b * query_rows).astype(jnp.int32)
        q_block = lax.dynamic_slice_in_dim(q_heads, first, query_rows, 0)
        q_pos = first + jnp.arange(query_rows, dtype=jnp.int32)
        q_doc = lax.dynamic_slice_in_dim(document, first, query_rows, 0)
        visible = (position[None, :] <= q_pos[:, None]) & (document[None, :] == q_doc[:, None])

        def per_head(h):
            q_one = q_block[:, h].astype(jnp.float32)
            k_one = k_heads[:, h].astype(jnp.float32)
            v_one = v_heads[:, h].astype(jnp.float32)
            scores = jnp.einsum('tgd,sd->gts', q_one, k_one) * factor
            scores = jnp.where(visible[None], scores, -1e30)
            top = jnp.max(scores, axis=-1, keepdims=True)
            expo = jnp.where(visible[None], jnp.exp(scores - top), 0.0)
            totals = jnp.sum(expo, axis=-1)
            weights = expo.astype(jnp.bfloat16).astype(jnp.float32)
            summed = jnp.einsum('gts,sd->tgd', weights, v_one)
            return summed / jnp.transpose(totals)[:, :, None]

        result = lax.map(per_head, jnp.arange(KVHEADS, dtype=jnp.int32))
        return jnp.transpose(result, (1, 0, 2, 3)).reshape(query_rows, QHEADS * HD)

    attended = lax.map(per_block, jnp.arange(SEQ // query_rows, dtype=jnp.int32))
    attended = attended.reshape(SEQ, QHEADS * HD).astype(jnp.bfloat16)
    return jnp.dot(attended, out_weight, preferred_element_type=jnp.float32).astype(jnp.bfloat16)
```

```python
import functools

import jax
import jax.numpy as jnp
from jax import lax
from jax.experimental import pallas as pl
from jax.experimental.pallas import tpu as pltpu
from jax.sharding import PartitionSpec as P

HD = 128
BLOCK = 128
NX, NY, NZ, NC = 4, 2, 4, 2
ROWS = 256
SEQ = 16384
GROUP = 6
PIECE = ROWS // NX
QW = GROUP * HD
CHUNK = 512
MESH = pl.DeviceIdType.MESH
VMEM = pl.BlockSpec(memory_space=pltpu.VMEM)
ANY = pl.BlockSpec(memory_space=pl.ANY)


def place():
    x = lax.axis_index("inner")
    outer = lax.axis_index("outer")
    return x, outer // (NZ * NC), (outer // NC) % NZ, outer % NC


def at(x, y, z, c):
    return {"inner": x, "outer": y * (NZ * NC) + z * NC + c}


def turn(i, n, d):
    return (i + n + d) % n


def greet(others):
    barrier = pltpu.get_barrier_semaphore()
    for other in others:
        pl.semaphore_signal(barrier, inc=1, device_id=other, device_id_type=MESH)
    pl.semaphore_wait(barrier, len(others))


def remote(src, dst, send, recv, to):
    return pltpu.make_async_remote_copy(
        src_ref=src, dst_ref=dst, send_sem=send, recv_sem=recv, device_id=to, device_id_type=MESH
    )


def convolve(halo, field, taps, out, width, tile):
    def one(i, carry):
        cols = pl.ds(pl.multiple_of(i * tile, tile), tile)
        wide = jnp.concatenate(
            [halo[:, cols].astype(jnp.float32), field[:, cols].astype(jnp.float32)], axis=0
        )
        total = taps[0:1, cols] * wide[16:]
        for j in range(1, 4):
            total = total + taps[j : j + 1, cols] * wide[16 - j : 16 - j + ROWS]
        out[:, cols] = total.astype(jnp.bfloat16)
        return carry

    lax.fori_loop(0, width // tile, one, 0)


def gather_kernel(
    q_ref, k_ref, v_ref, qt_ref, kt_ref, qx_ref, gk_ref, gv_ref,
    halo_q, halo_k, cq, ck, halo_s, halo_r, y_s, y_r, own_s, q_s, q_r, q_own, send, recv,
):
    x, y, z, c = place()
    shard = x * 16 + lax.axis_index("outer")
    after = turn(shard, 64, 1)
    before = turn(shard, 64, -1)
    nxt = {"inner": after // 16, "outer": after % 16}
    prv = {"inner": before // 16, "outer": before % 16}
    across = at(x, 1 - y, z, c)
    sibling = at(x, y, z, 1 - c)
    steps = {
        "z": (at(x, y, turn(z, NZ, 1), c), at(x, y, turn(z, NZ, -1), c)),
        "x": (at(turn(x, NX, 1), y, z, c), at(turn(x, NX, -1), y, z, c)),
    }
    peers = [
        (dx, dy) for dx in (0, 1, -1, 2) for dy in (0, 1) if (dx, dy) != (0, 0)
    ]
    peer_ids = [at(turn(x, NX, dx), (y + dy) % 2, z, c) for dx, dy in peers]
    greet(
        [nxt, prv, across, sibling, *steps["z"], *steps["x"]]
        + [d for d, (dx, dy) in zip(peer_ids, peers) if dx == 2 or dy == 1 and dx != 0]
    )

    halos = [
        remote(k_ref.at[pl.ds(ROWS - 16, 16)], halo_k, halo_s.at[0], halo_r.at[0], nxt),
        remote(q_ref.at[pl.ds(ROWS - 16, 16)], halo_q, halo_s.at[1], halo_r.at[1], nxt),
    ]
    for copy in halos:
        copy.start()

    mine = pl.ds(pl.multiple_of(y * HD, HD), HD)
    theirs = pl.ds(pl.multiple_of((1 - y) * HD, HD), HD)

    def spread(part, source, full):
        out = remote(source.at[:, theirs], full.at[x, y, z, c], y_s.at[part], y_r.at[part], across)
        out.start()
        own = pltpu.make_async_copy(source.at[:, mine], full.at[x, y, z, c], own_s.at[part])
        own.start()
        return out, own

    v_y = spread(1, v_ref, gv_ref)
    halos[0].wait_recv()

    @pl.when(shard == 0)
    def _():
        halo_k[...] = jnp.zeros_like(halo_k)

    convolve(halo_k, k_ref, kt_ref, ck, 2 * HD, 128)
    k_y = spread(0, ck, gk_ref)

    class Part:
        pass

    parts = []
    for index, full, first, second in ((0, gk_ref, "z", "x"), (1, gv_ref, "x", "z")):
        part = Part()
        part.index, part.full, part.first, part.second = index, full, steps[first], steps[second]
        part.swap = first == "x"
        part.sends = []
        part.used = 0
        parts.append(part)

    def block(part, da, db, half=None):
        xx, zz = (turn(x, NX, da), turn(z, NZ, db)) if part.swap else (turn(x, NX, db), turn(z, NZ, da))
        rows = pl.ds(0, NY) if half is None else half
        return part.full.at[xx, rows, zz, c]

    def push(part, ref, to, slot):
        copy = remote(ref, ref, send.at[part.index, slot], recv.at[part.index, slot], to)
        copy.start()
        part.sends.append(copy)

    def landed(part, ref, slot):
        remote(ref, ref, send.at[part.index, slot], recv.at[part.index, slot], across).wait_recv()

    offsets = (0, -1, 1, 2)
    def to_sibling(part, da, db):
        push(part, block(part, da, db), sibling, 20 + offsets.index(da) * 4 + offsets.index(db))

    def second_ring(part, da):
        k = offsets.index(da)
        for side in range(2):
            push(part, block(part, da, 0), part.second[side], 4 + 2 * k + side)
        to_sibling(part, da, 0)

    for part, (out, own) in ((parts[1], v_y), (parts[0], k_y)):
        out.wait_recv()
        own.wait()
        for side in range(2):
            push(part, block(part, 0, 0), part.first[side], side)
        second_ring(part, 0)

    halos[1].wait_recv()

    @pl.when(shard == 0)
    def _():
        halo_q[...] = jnp.zeros_like(halo_q)

    convolve(halo_q, q_ref, qt_ref, cq, 2 * QW, 128)

    q_copies = []
    for i, ((dx, dy), to) in enumerate(zip(peers, peer_ids)):
        px, py = turn(x, NX, dx), (y + dy) % 2
        piece = cq.at[
            pl.ds(pl.multiple_of(px * PIECE, PIECE), PIECE), pl.ds(pl.multiple_of(py * QW, QW), QW)
        ]
        copy = remote(piece, qx_ref.at[x, y], q_s.at[i], q_r.at[i], to)
        copy.start()
        q_copies.append(copy)
    own_q = pltpu.make_async_copy(
        cq.at[
            pl.ds(pl.multiple_of(x * PIECE, PIECE), PIECE), pl.ds(pl.multiple_of(y * QW, QW), QW)
        ],
        qx_ref.at[x, y],
        q_own,
    )
    own_q.start()

    for part in parts:
        landed(part, block(part, -1, 0), 0)
        push(part, block(part, -1, 0, 0), part.first[0], 2)
        second_ring(part, -1)
        landed(part, block(part, 1, 0), 1)
        push(part, block(part, 1, 0, 1), part.first[1], 3)
        second_ring(part, 1)
    for part in parts:
        landed(part, block(part, 2, 0, 0), 2)
        landed(part, block(part, 2, 0, 1), 3)
        second_ring(part, 2)
    for k, da in enumerate(offsets):
        for part in parts:
            landed(part, block(part, da, -1), 4 + 2 * k)
            push(part, block(part, da, -1, 0), part.second[0], 12 + 2 * k)
            to_sibling(part, da, -1)
            landed(part, block(part, da, 1), 5 + 2 * k)
            push(part, block(part, da, 1, 1), part.second[1], 13 + 2 * k)
            to_sibling(part, da, 1)
    for k, da in enumerate(offsets):
        for part in parts:
            landed(part, block(part, da, 2, 0), 12 + 2 * k)
            landed(part, block(part, da, 2, 1), 13 + 2 * k)
            to_sibling(part, da, 2)

    for part in parts:
        for copy in part.sends:
            copy.wait_send()
        for i, da in enumerate(offsets):
            for j, db in enumerate(offsets):
                xx, zz = (turn(x, NX, da), turn(z, NZ, db)) if part.swap else (turn(x, NX, db), turn(z, NZ, da))
                landed(part, part.full.at[xx, pl.ds(0, NY), zz, 1 - c], 20 + 4 * i + j)
    for copy in halos:
        copy.wait_send()
    for out, own in (v_y, k_y):
        out.wait_send()
    for i, (dx, dy) in enumerate(peers):
        q_copies[i].wait_send()
        ref = qx_ref.at[turn(x, NX, -dx), (y + dy) % 2]
        remote(ref, ref, q_s.at[i], q_r.at[i], across).wait_recv()
    own_q.wait()


def attend_kernel(first_ref, limit_ref, q_ref, gk_ref, gv_ref, o_ref, keys, values, q_all, m_s, acc_s, sems):
    loads = []
    for x in range(NX):
        rows = pl.ds(x * (SEQ // NX), SEQ // NX)
        for i, (src, dst) in enumerate(((gk_ref, keys), (gv_ref, values))):
            copy = pltpu.make_async_copy(src.at[rows], dst.at[rows], sems.at[i, x])
            copy.start()
            loads.append(copy)
    keys[SEQ:, :] = jnp.zeros((CHUNK, HD), jnp.bfloat16)
    values[SEQ:, :] = jnp.zeros((CHUNK, HD), jnp.bfloat16)
    factor = HD**-0.5 * 1.4426950408889634
    stack = GROUP * PIECE
    split = 2
    part_rows = stack // split
    ones = jnp.ones((CHUNK, HD), jnp.bfloat16)

    for copy in loads:
        copy.wait()

    def position(p, carry):
        first = first_ref[p]
        limit = limit_ref[p]
        count = (limit - first + CHUNK - 1) // CHUNK
        for h in range(GROUP):
            q_all[h * PIECE : (h + 1) * PIECE, :] = q_ref[p, :, h * HD : (h + 1) * HD]
        m_s[...] = jnp.full_like(m_s, -1e30)
        acc_s[...] = jnp.zeros_like(acc_s)

        def step(i, masked):
            start = pl.multiple_of(first + i * CHUNK, BLOCK)
            k = keys[pl.ds(start, CHUNK), :]
            v = jnp.concatenate([values[pl.ds(start, CHUNK), :], ones], axis=1)
            for r in range(split):
                rows = pl.ds(r * part_rows, part_rows)
                s = lax.dot_general(
                    q_all[rows, :], k, (((1,), (1,)), ((), ())), preferred_element_type=jnp.float32
                )
                if masked:
                    token = limit - PIECE + lax.rem(
                        lax.broadcasted_iota(jnp.int32, (part_rows, CHUNK), 0), PIECE
                    )
                    key = start + lax.broadcasted_iota(jnp.int32, (part_rows, CHUNK), 1)
                    s = jnp.where(key <= token, s, -1e30)
                old = m_s[rows, :]
                top = jnp.maximum(old, jnp.max(s, axis=1, keepdims=True))
                decay = jnp.exp2((old - top) * factor)
                weights = jnp.exp2((s - top[:, :1]) * factor).astype(jnp.bfloat16)
                added = jnp.dot(weights, v, preferred_element_type=jnp.float32)
                m_s[rows, :] = top
                acc_s[rows, :] = acc_s[rows, :] * jnp.concatenate([decay, decay], axis=1) + added

        def body(i, carry):
            step(i, False)
            return carry

        lax.fori_loop(0, count - 1, body, 0)
        step(count - 1, True)
        for h in range(GROUP):
            rows = slice(h * PIECE, (h + 1) * PIECE)
            o_ref[p, :, h * HD : (h + 1) * HD] = (
                acc_s[rows, :HD] / acc_s[rows, HD:]
            ).astype(jnp.bfloat16)
        return carry

    lax.fori_loop(0, NX * NY, position, 0)


TILE = 512


def project_kernel(o_ref, w_ref, out_ref, full, w_all, sent, got, own, r_s, r_r, r_own, w_s, c_s, c_r):
    x, y, z, c = place()
    head = lax.axis_index("head")
    half = w_ref.shape[1] // 2
    tiles = half // TILE
    peers = [
        (dx, dy) for dx in (0, 1, -1, 2) for dy in (0, 1) if (dx, dy) != (0, 0)
    ]
    peer_ids = [at(turn(x, NX, dx), (y + dy) % 2, z, c) for dx, dy in peers]
    partner = {"head": 1 - head}

    def w_copy(t):
        side = jnp.where(t < tiles, 1 - head, head)
        column = side * half + (t % tiles) * TILE
        return pltpu.make_async_copy(
            w_ref.at[:, pl.ds(pl.multiple_of(column, TILE), TILE)], w_all.at[t], w_s.at[t]
        )

    for t in range(2 * tiles):
        w_copy(t).start()
    greet(peer_ids + [partner])

    def spot(xx, yy):
        return full.at[
            pl.ds(pl.multiple_of(xx * PIECE, PIECE), PIECE), pl.ds(pl.multiple_of(yy * QW, QW), QW)
        ]

    back = []
    for i, ((dx, dy), to) in enumerate(zip(peers, peer_ids)):
        copy = remote(
            o_ref.at[turn(x, NX, dx), (y + dy) % 2], spot(x, y), r_s.at[i], r_r.at[i], to
        )
        copy.start()
        back.append(copy)
    mine = pltpu.make_async_copy(o_ref.at[x, y], spot(x, y), r_own)
    mine.start()
    mine.wait()
    for i, (dx, dy) in enumerate(peers):
        ref = spot(turn(x, NX, -dx), (y + dy) % 2)
        remote(ref, ref, r_s.at[i], r_r.at[i], partner).wait_recv()

    def cross(t):
        return remote(sent.at[t], got.at[t], c_s.at[t], c_r.at[t], partner)

    def first(t, carry):
        w_copy(t).wait()
        sent[t] = jnp.dot(full[...], w_all[t], preferred_element_type=jnp.float32).astype(jnp.bfloat16)
        cross(t).start()
        return carry

    lax.fori_loop(0, tiles, first, 0)

    def second(t, carry):
        w_copy(t + tiles).wait()
        own[t] = jnp.dot(full[...], w_all[t + tiles], preferred_element_type=jnp.float32)
        return carry

    lax.fori_loop(0, tiles, second, 0)

    def last(t, carry):
        cross(t).wait_recv()
        out_ref[:, pl.ds(pl.multiple_of(t * TILE, TILE), TILE)] = (
            own[t] + got[t].astype(jnp.float32)
        ).astype(jnp.bfloat16)
        return carry

    lax.fori_loop(0, tiles, last, 0)

    def finish(t, carry):
        cross(t).wait_send()
        return carry

    lax.fori_loop(0, tiles, finish, 0)
    for copy in back:
        copy.wait_send()


def local(queries, key_vectors, value_vectors, query_taps, key_taps, out_weight, doc_blocks):
    bf16 = jnp.bfloat16
    dma = pltpu.SemaphoreType.DMA
    shape = jax.ShapeDtypeStruct
    qx, gk, gv = pl.pallas_call(
        gather_kernel,
        out_shape=(
            shape((NX, NY, PIECE, QW), bf16),
            shape((NX, NY, NZ, NC, ROWS, HD), bf16),
            shape((NX, NY, NZ, NC, ROWS, HD), bf16),
        ),
        in_specs=[VMEM] * 5,
        out_specs=(ANY, ANY, ANY),
        scratch_shapes=[
            pltpu.VMEM((16, 2 * QW), bf16),
            pltpu.VMEM((16, 2 * HD), bf16),
            pltpu.VMEM((ROWS, 2 * QW), bf16),
            pltpu.VMEM((ROWS, 2 * HD), bf16),
            dma((2,)), dma((2,)), dma((2,)), dma((2,)), dma((2,)),
            dma((7,)), dma((7,)), dma,
            dma((2, 36)), dma((2, 36)),
        ],
        compiler_params=pltpu.CompilerParams(
            collective_id=0, has_side_effects=True, vmem_limit_bytes=32 << 20
        ),
        name="gather",
    )(queries, key_vectors, value_vectors, query_taps, key_taps)

    starts = (jnp.cumsum(doc_blocks) - doc_blocks) * BLOCK
    x = lax.axis_index("inner")
    outer = lax.axis_index("outer")
    spots = jnp.arange(NX * NY, dtype=jnp.int32)
    tokens = ((spots // NY) * 16 + (spots % NY) * 8 + outer % 8) * ROWS + x * PIECE
    first = jnp.max(jnp.where(starts[None, :] <= tokens[:, None], starts[None, :], 0), axis=1)
    smem = pl.BlockSpec(memory_space=pltpu.SMEM)
    attended = pl.pallas_call(
        attend_kernel,
        out_shape=shape((NX * NY, PIECE, QW), bf16),
        in_specs=[smem, smem, VMEM, ANY, ANY],
        out_specs=VMEM,
        scratch_shapes=[
            pltpu.VMEM((SEQ + CHUNK, HD), bf16),
            pltpu.VMEM((SEQ + CHUNK, HD), bf16),
            pltpu.VMEM((GROUP * PIECE, HD), bf16),
            pltpu.VMEM((GROUP * PIECE, HD), jnp.float32),
            pltpu.VMEM((GROUP * PIECE, 2 * HD), jnp.float32),
            dma((2, NX)),
        ],
        compiler_params=pltpu.CompilerParams(vmem_limit_bytes=48 << 20),
        name="attend",
    )(
        first.astype(jnp.int32),
        (tokens + PIECE).astype(jnp.int32),
        qx.reshape(NX * NY, PIECE, QW),
        gk.reshape(SEQ, HD),
        gv.reshape(SEQ, HD),
    )

    model = out_weight.shape[1]
    tiles = model // 2 // TILE
    return pl.pallas_call(
        project_kernel,
        out_shape=shape((ROWS, model // 2), bf16),
        in_specs=[ANY, ANY],
        out_specs=VMEM,
        scratch_shapes=[
            pltpu.VMEM((ROWS, 2 * QW), bf16),
            pltpu.VMEM((2 * tiles, 2 * QW, TILE), bf16),
            pltpu.VMEM((tiles, ROWS, TILE), bf16),
            pltpu.VMEM((tiles, ROWS, TILE), bf16),
            pltpu.VMEM((tiles, ROWS, TILE), jnp.float32),
            dma((7,)), dma((7,)), dma,
            dma((2 * tiles,)), dma((tiles,)), dma((tiles,)),
        ],
        compiler_params=pltpu.CompilerParams(
            collective_id=1, has_side_effects=True, vmem_limit_bytes=48 << 20
        ),
        name="project",
    )(attended.reshape(NX, NY, PIECE, QW), out_weight)


def solution(mesh):
    in_specs = (
        P(("inner", "outer"), "head"),
        P(("inner", "outer"), "head"),
        P(("inner", "outer"), "head"),
        P(None, "head"),
        P(None, "head"),
        P("head", None),
        P(),
    )
    out_specs = P(("inner", "outer"), "head")
    return jax.shard_map(local, mesh=mesh, in_specs=in_specs, out_specs=out_specs, check_vma=False)
```

```python
import functools

import jax
import jax.numpy as jnp
from jax import lax
from jax.experimental import pallas as pl
from jax.experimental.pallas import tpu as pltpu
from jax.sharding import PartitionSpec as P

HD = 128
BLOCK = 128
NX, NY, NZ, NC = 4, 2, 4, 2
ROWS = 256
SEQ = 16384
GROUP = 6
PIECE = ROWS // NX
QW = GROUP * HD
CHUNK = 1024
LIMIT = 2.0**60
MESH = pl.DeviceIdType.MESH
VMEM = pl.BlockSpec(memory_space=pltpu.VMEM)
ANY = pl.BlockSpec(memory_space=pl.ANY)


def place():
    x = lax.axis_index("inner")
    outer = lax.axis_index("outer")
    return x, outer // (NZ * NC), (outer // NC) % NZ, outer % NC


def at(x, y, z, c):
    return {"inner": x, "outer": y * (NZ * NC) + z * NC + c}


def turn(i, n, d):
    return (i + n + d) % n


def share(x, z, c):
    quarter = (2 * x + z) % 4
    return pl.ds(pl.multiple_of(quarter * 384 + c * 192, 192), 192)


def greet(others):
    barrier = pltpu.get_barrier_semaphore()
    for other in others:
        pl.semaphore_signal(barrier, inc=1, device_id=other, device_id_type=MESH)
    pl.semaphore_wait(barrier, len(others))


def remote(src, dst, send, recv, to):
    return pltpu.make_async_remote_copy(
        src_ref=src, dst_ref=dst, send_sem=send, recv_sem=recv, device_id=to, device_id_type=MESH
    )


def convolve(halo, field, taps, out, width, tile):
    def one(i, carry):
        cols = pl.ds(pl.multiple_of(i * tile, tile), tile)
        wide = jnp.concatenate(
            [halo[:, cols].astype(jnp.float32), field[:, cols].astype(jnp.float32)], axis=0
        )
        total = taps[0:1, cols] * wide[16:]
        for j in range(1, 4):
            total = total + taps[j : j + 1, cols] * wide[16 - j : 16 - j + ROWS]
        out[:, cols] = total.astype(jnp.bfloat16)
        return carry

    lax.fori_loop(0, width // tile, one, 0)


def gather_kernel(
    q_hbm, k_hbm, v_hbm, qt_hbm, kt_hbm, w_hbm, qx_ref, gk_ref, gv_ref, w_ref,
    q_ref, k_ref, v_ref, qt_ref, kt_ref,
    halo_q, halo_k, cq, ck, vt, load_s, halo_s, halo_r, y_s, y_r, own_s, q_s, q_r, q_own, w_s, w_r, send, recv,
):
    x, y, z, c = place()
    head = lax.axis_index("head")
    loads = [
        pltpu.make_async_copy(src, dst, load_s.at[i])
        for i, (src, dst) in enumerate(
            ((k_hbm, k_ref), (v_hbm, v_ref), (kt_hbm, kt_ref), (q_hbm, q_ref), (qt_hbm, qt_ref))
        )
    ]
    for load in loads:
        load.start()
    shard = x * 16 + lax.axis_index("outer")
    after = turn(shard, 64, 1)
    before = turn(shard, 64, -1)
    nxt = {"inner": after // 16, "outer": after % 16}
    prv = {"inner": before // 16, "outer": before % 16}
    across = at(x, 1 - y, z, c)
    opposite = {"head": 1 - head, **across}
    sibling = at(x, y, z, 1 - c)
    steps = {
        "z": (at(x, y, turn(z, NZ, 1), c), at(x, y, turn(z, NZ, -1), c)),
        "x": (at(turn(x, NX, 1), y, z, c), at(turn(x, NX, -1), y, z, c)),
    }
    peers = [
        (dx, dy) for dx in (0, 1, -1, 2) for dy in (0, 1) if (dx, dy) != (0, 0)
    ]
    peer_ids = [at(turn(x, NX, dx), (y + dy) % 2, z, c) for dx, dy in peers]
    greet(
        [nxt, prv, across, opposite, sibling, *steps["z"], *steps["x"]]
        + [d for d, (dx, dy) in zip(peer_ids, peers) if dx == 2 or dy == 1 and dx != 0]
    )

    halos = [
        remote(k_hbm.at[pl.ds(ROWS - 16, 16)], halo_k, halo_s.at[0], halo_r.at[0], nxt),
        remote(q_hbm.at[pl.ds(ROWS - 16, 16)], halo_q, halo_s.at[1], halo_r.at[1], nxt),
    ]
    for copy in halos:
        copy.start()

    mine = pl.ds(pl.multiple_of(y * HD, HD), HD)
    theirs = pl.ds(pl.multiple_of((1 - y) * HD, HD), HD)

    class Part:
        pass

    parts = []
    for index, (full, size, block_y, first, second) in enumerate((
        (gv_ref, HD, y, "x", "z"),
        (gk_ref, ROWS, y, "z", "x"),
        (gv_ref, HD, 1 - y, "x", "z"),
        (gk_ref, ROWS, 1 - y, "x", "z"),
    )):
        part = Part()
        part.index, part.full, part.size, part.y = index, full, size, block_y
        part.first, part.second = steps[first], steps[second]
        part.swap = first == "x"
        part.sends = []
        parts.append(part)
    v_mine, k_mine, v_theirs, k_theirs = parts

    def block(part, da, db, half=None, core=c):
        xx, zz = (turn(x, NX, da), turn(z, NZ, db)) if part.swap else (turn(x, NX, db), turn(z, NZ, da))
        rows = pl.ds(0, part.size) if half is None else pl.ds(half * part.size // 2, part.size // 2)
        return part.full.at[xx, part.y, zz, core, rows]

    def push(part, ref, to, slot, src=None):
        copy = remote(ref if src is None else src, ref, send.at[part.index, slot], recv.at[part.index, slot], to)
        copy.start()
        part.sends.append(copy)

    def landed(part, ref, slot):
        remote(ref, ref, send.at[part.index, slot], recv.at[part.index, slot], across).wait_recv()

    offsets = (0, -1, 1, 2)
    def to_sibling(part, da, db, src=None):
        push(part, block(part, da, db), sibling, 20 + offsets.index(da) * 4 + offsets.index(db), src)

    def second_ring(part, da, src=None):
        k = offsets.index(da)
        for side in range(2):
            push(part, block(part, da, 0), part.second[side], 4 + 2 * k + side, src)
        to_sibling(part, da, 0, src)

    def begin(part, src=None):
        for side in range(2):
            push(part, block(part, 0, 0), part.first[side], side, src)
        second_ring(part, 0, src)

    def ring_step(part):
        landed(part, block(part, -1, 0), 0)
        push(part, block(part, -1, 0, 0), part.first[0], 2)
        landed(part, block(part, 1, 0), 1)
        push(part, block(part, 1, 0, 1), part.first[1], 3)
        second_ring(part, -1)
        second_ring(part, 1)

    def ring_end(part):
        landed(part, block(part, 2, 0, 0), 2)
        landed(part, block(part, 2, 0, 1), 3)
        second_ring(part, 2)

    def pass_on(part, da):
        k = offsets.index(da)
        landed(part, block(part, da, -1), 4 + 2 * k)
        push(part, block(part, da, -1, 0), part.second[0], 12 + 2 * k)
        landed(part, block(part, da, 1), 5 + 2 * k)
        push(part, block(part, da, 1, 1), part.second[1], 13 + 2 * k)
        to_sibling(part, da, -1)
        to_sibling(part, da, 1)

    def finish(part, da):
        k = offsets.index(da)
        landed(part, block(part, da, 2, 0), 12 + 2 * k)
        landed(part, block(part, da, 2, 1), 13 + 2 * k)
        to_sibling(part, da, 2)

    def to_across(part, src):
        copy = remote(src, part.full.at[x, y, z, c], y_s.at[part.index], y_r.at[part.index], across)
        copy.start()
        part.sends.append(copy)

    def from_across(part, source):
        ref = block(part, 0, 0)
        remote(ref, ref, y_s.at[source.index], y_r.at[source.index], across).wait_recv()

    def keep(part, src):
        part.own = pltpu.make_async_copy(src, block(part, 0, 0), own_s.at[part.index])
        part.own.start()

    loads[1].wait()
    vt[...] = v_ref[...].T
    to_across(v_mine, vt.at[theirs])
    begin(v_mine, vt.at[mine])
    keep(v_mine, vt.at[mine])

    loads[0].wait()
    loads[2].wait()
    halos[0].wait_recv()

    @pl.when(shard == 0)
    def _():
        halo_k[...] = jnp.zeros_like(halo_k)

    convolve(halo_k, k_ref, kt_ref, ck, 2 * HD, 128)
    to_across(k_mine, ck.at[:, theirs])
    begin(k_mine, ck.at[:, mine])
    keep(k_mine, ck.at[:, mine])

    from_across(v_theirs, v_mine)
    begin(v_theirs)
    ring_step(v_mine)
    from_across(k_theirs, k_mine)
    begin(k_theirs)
    ring_step(k_mine)

    half = w_hbm.shape[1] // 2
    w_copy = remote(
        w_hbm.at[share(x, z, c), pl.ds(pl.multiple_of((1 - head) * half, half), half)],
        w_ref, w_s, w_r, opposite,
    )
    w_copy.start()

    loads[3].wait()
    loads[4].wait()
    halos[1].wait_recv()

    @pl.when(shard == 0)
    def _():
        halo_q[...] = jnp.zeros_like(halo_q)

    convolve(halo_q, q_ref, qt_ref, cq, 2 * QW, 128)

    q_copies = []
    for i, ((dx, dy), to) in enumerate(zip(peers, peer_ids)):
        px, py = turn(x, NX, dx), (y + dy) % 2
        piece = cq.at[
            pl.ds(pl.multiple_of(px * PIECE, PIECE), PIECE), pl.ds(pl.multiple_of(py * QW, QW), QW)
        ]
        copy = remote(piece, qx_ref.at[x, y], q_s.at[i], q_r.at[i], to)
        copy.start()
        q_copies.append(copy)
    own_q = pltpu.make_async_copy(
        cq.at[
            pl.ds(pl.multiple_of(x * PIECE, PIECE), PIECE), pl.ds(pl.multiple_of(y * QW, QW), QW)
        ],
        qx_ref.at[x, y],
        q_own,
    )
    own_q.start()

    ring_end(v_mine)
    ring_step(v_theirs)
    ring_end(k_mine)
    ring_step(k_theirs)
    ring_end(v_theirs)
    ring_end(k_theirs)
    for da in offsets:
        for part in parts:
            pass_on(part, da)
    for da in offsets:
        for part in parts:
            finish(part, da)

    for part in parts:
        for copy in part.sends:
            copy.wait_send()
        for i, da in enumerate(offsets):
            for j, db in enumerate(offsets):
                landed(part, block(part, da, db, core=1 - c), 20 + 4 * i + j)
    v_mine.own.wait()
    k_mine.own.wait()
    for copy in halos:
        copy.wait_send()
    for i, (dx, dy) in enumerate(peers):
        q_copies[i].wait_send()
        ref = qx_ref.at[turn(x, NX, -dx), (y + dy) % 2]
        remote(ref, ref, q_s.at[i], q_r.at[i], across).wait_recv()
    own_q.wait()
    w_copy.wait()


def find_spans(doc_ref, first_ref, limit_ref):
    x = lax.axis_index("inner")
    outer = lax.axis_index("outer")
    for p in range(NX * NY):
        token = ((p // NY) * 16 + (p % NY) * 8 + outer % 8) * ROWS + x * PIECE
        start = jnp.int32(0)
        first = jnp.int32(0)
        for d in range(doc_ref.shape[0]):
            first = jnp.where(start <= token, start, first)
            start = start + doc_ref[d] * BLOCK
        first_ref[p] = first
        limit_ref[p] = token + PIECE


def attend_kernel(doc_ref, q_ref, gk_ref, gv_ref, o_ref, first_ref, limit_ref, keys, values, q_all, q_t, acc, add, l_s, l_n, m_s, q_sem, k_sem, v_sem):
    def key_load(i):
        rows = pl.ds(pl.multiple_of(i * CHUNK, CHUNK), CHUNK)
        return pltpu.make_async_copy(gk_ref.at[rows], keys.at[rows], k_sem.at[i])

    def value_load(i):
        columns = pl.ds(pl.multiple_of(i * ROWS, ROWS), ROWS)
        return pltpu.make_async_copy(gv_ref.at[i], values.at[:, columns], v_sem.at[i])

    def start_loads(i, carry):
        key_load(i).start()
        for u in range(CHUNK // ROWS):
            value_load(i * (CHUNK // ROWS) + u).start()
        return carry

    q_load = pltpu.make_async_copy(q_ref, q_all, q_sem)
    q_load.start()
    lax.fori_loop(0, SEQ // CHUNK, start_loads, 0)
    find_spans(doc_ref, first_ref, limit_ref)
    keys[SEQ:, :] = jnp.zeros((ROWS, HD), jnp.bfloat16)
    values[:, SEQ:] = jnp.zeros((HD, ROWS), jnp.bfloat16)
    q_load.wait()
    for p in range(NX * NY):
        for h in range(GROUP):
            q_t[p, :, h * PIECE : (h + 1) * PIECE] = q_all[p, :, h * HD : (h + 1) * HD].T

    def wait_loads(i, carry):
        key_load(i).wait()
        for u in range(CHUNK // ROWS):
            value_load(i * (CHUNK // ROWS) + u).wait()
        return carry

    lax.fori_loop(0, SEQ // CHUNK, wait_loads, 0)
    factor = HD**-0.5 * 1.4426950408889634
    width = GROUP * PIECE

    def position(p, carry):
        first = first_ref[p]
        limit = limit_ref[p]
        pieces = (limit - first + ROWS - 1) // ROWS
        count = (pieces - 1) // (CHUNK // ROWS)
        rest = pieces - count * (CHUNK // ROWS)

        def scores(start, size):
            return jnp.dot(keys[pl.ds(start, size), :], q_t[p], preferred_element_type=jnp.float32)

        def mix(start, size, weights):
            return jnp.dot(values[:, pl.ds(start, size)], weights, preferred_element_type=jnp.float32)

        def add_up(exps, size):
            return jnp.sum(exps.reshape(size // 8, 8, width), axis=0)

        def tail(size):
            start = pl.multiple_of(first + count * CHUNK, BLOCK)
            s = scores(start, size)
            token = limit - PIECE + lax.rem(
                lax.broadcasted_iota(jnp.int32, (ROWS, width), 1), PIECE
            )
            key = start + size - ROWS + lax.broadcasted_iota(jnp.int32, (ROWS, width), 0)
            edge = jnp.where(key <= token, s[size - ROWS :], -1e30)
            s = edge if size == ROWS else jnp.concatenate([s[: size - ROWS], edge], axis=0)
            top = jnp.max(s, axis=0, keepdims=True)
            exps = jnp.exp2((s - top) * factor)
            l_s[...] = add_up(exps, size)
            m_s[...] = jnp.broadcast_to(top, m_s.shape)
            acc[...] = mix(start, size, exps.astype(jnp.bfloat16))

        for k in range(1, CHUNK // ROWS + 1):
            pl.when(rest == k)(functools.partial(tail, k * ROWS))

        def chunk(i, carry):
            start = pl.multiple_of(first + i * CHUNK, BLOCK)
            exps = jnp.exp2((scores(start, CHUNK) - m_s[0:1, :]) * factor)
            totals = l_s[...] + add_up(exps, CHUNK)
            add[...] = mix(start, CHUNK, exps.astype(jnp.bfloat16))
            l_n[...] = totals
            high = jnp.logical_not(jnp.max(totals) <= LIMIT)

            @pl.when(jnp.logical_not(high))
            def _():
                acc[...] = acc[...] + add[...]
                l_s[...] = l_n[...]

            @pl.when(high)
            def _():
                s = scores(start, CHUNK)
                old = m_s[0:1, :]
                top = jnp.maximum(old, jnp.max(s, axis=0, keepdims=True))
                decay = jnp.exp2((old - top) * factor)
                exps = jnp.exp2((s - top) * factor)
                l_s[...] = l_s[...] * decay + add_up(exps, CHUNK)
                m_s[...] = jnp.broadcast_to(top, m_s.shape)
                acc[...] = acc[...] * decay + mix(start, CHUNK, exps.astype(jnp.bfloat16))

            return carry

        lax.fori_loop(0, count, chunk, 0)
        totals = jnp.sum(l_s[...], axis=0, keepdims=True)
        result = (acc[...] / totals).T
        for h in range(GROUP):
            o_ref[p, :, h * HD : (h + 1) * HD] = result[h * PIECE : (h + 1) * PIECE].astype(
                jnp.bfloat16
            )
        return carry

    lax.fori_loop(0, NX * NY, position, 0)


TILE = 512


def project_kernel(
    o_ref, w_ref, share_ref, out_ref, full, other, w_own, w_far, total,
    x_s, x_r, o_s, y_s, y_r, w_s, own_s, send, recv,
):
    x, y, z, c = place()
    head = lax.axis_index("head")
    group = 2 * head + y
    half = w_ref.shape[1] // 2
    tiles = half // TILE
    sibling = at(x, y, z, 1 - c)
    z_ids = [at(x, y, turn(z, NZ, d), c) for d in (1, -1)]
    x_ids = [at(turn(x, NX, d), y, z, c) for d in (1, -1, 2)]
    across = at(x, 1 - y, z, c)
    y_ids = [across, {"head": 1 - head, **across}, {"head": 1 - head, **at(x, y, z, c)}]

    w_load = pltpu.make_async_copy(
        w_ref.at[:, pl.ds(pl.multiple_of(head * half, half), half)], w_own, w_s
    )
    greet([sibling, *z_ids, *x_ids, *y_ids])

    def piece(xx):
        return pl.ds(pl.multiple_of(xx * PIECE, PIECE), PIECE)

    here = piece(x)
    x_copies = []
    for i, (d, to) in enumerate(zip((1, -1, 2), x_ids)):
        xx = turn(x, NX, d)
        for j, copy in enumerate((
            remote(o_ref.at[xx, 1 - y], other.at[here], x_s.at[i, 0], x_r.at[i, 0], to),
            remote(o_ref.at[xx, y], full.at[group, here], x_s.at[i, 1], x_r.at[i, 1], to),
        )):
            copy.start()
            x_copies.append(copy)
    own_copies = [
        pltpu.make_async_copy(o_ref.at[x, 1 - y], other.at[here], o_s.at[0]),
        pltpu.make_async_copy(o_ref.at[x, y], full.at[group, here], o_s.at[1]),
    ]
    for copy in own_copies:
        copy.start()

    def rows_of(xx, zz, cc, start, size):
        quarter = (2 * xx + zz) % 4
        return pl.ds(pl.multiple_of(quarter * 384 + cc * 192 + start, 16), size)

    sent = []

    def push(src, dst, slot, to):
        copy = remote(src, dst, send.at[slot], recv.at[slot], to)
        copy.start()
        sent.append(copy)

    def landed(ref, slot):
        remote(ref, ref, send.at[slot], recv.at[slot], sibling).wait_recv()

    for k in range(2):
        mine = w_far.at[rows_of(x, z, c, 96 * k, 96)]
        from_share = share_ref.at[pl.ds(96 * k, 96)]
        for side in range(2):
            push(from_share, mine, 2 * k + side, z_ids[side])
    for side in range(2):
        push(
            share_ref.at[pl.ds(96 * side, 96)], w_far.at[rows_of(x, z, c, 96 * side, 96)], 4 + side, x_ids[side]
        )
    push(share_ref, w_far.at[rows_of(x, z, c, 0, 192)], 6, sibling)
    own_share = pltpu.make_async_copy(share_ref, w_far.at[rows_of(x, z, c, 0, 192)], own_s)
    own_share.start()
    w_load.start()

    y_copies = []

    def onward(i, xx):
        rows = piece(xx)
        for r, (src, to) in enumerate(
            zip((other.at[rows], other.at[rows], full.at[group, rows]), y_ids)
        ):
            copy = remote(src, full.at[group, rows], y_s.at[r, i], y_r.at[r, i], to)
            copy.start()
            y_copies.append(copy)

    for copy in own_copies:
        copy.wait()
    onward(3, x)
    for i, d in enumerate((1, -1, 2)):
        xx = turn(x, NX, -d)
        rows = piece(xx)
        remote(other.at[rows], other.at[rows], x_s.at[i, 0], x_r.at[i, 0], sibling).wait_recv()
        ref = full.at[group, rows]
        remote(ref, ref, x_s.at[i, 1], x_r.at[i, 1], sibling).wait_recv()
        onward(i, xx)

    def multiply(g, column, depth, w, row, first=False, last=False):
        def one(t, carry):
            cols = pl.ds(pl.multiple_of(t * TILE, TILE), TILE)
            value = jnp.dot(
                full[g, :, pl.ds(column, depth)], w[pl.ds(row, depth), cols], preferred_element_type=jnp.float32
            )
            if not first:
                value = value + total[t]
            if last:
                out_ref[:, cols] = value.astype(jnp.bfloat16)
            else:
                total[t] = value
            return carry

        lax.fori_loop(0, tiles, one, 0)

    w_load.wait()
    multiply(group, 0, QW, w_own, pl.multiple_of(y * QW, QW), first=True)

    def await_group(r, g):
        for i, d in enumerate((1, -1, 2, 0)):
            ref = full.at[g, piece(turn(x, NX, -d))]
            remote(ref, ref, y_s.at[r, i], y_r.at[r, i], sibling).wait_recv()

    await_group(0, group + 1 - 2 * y)
    multiply(group + 1 - 2 * y, 0, QW, w_own, pl.multiple_of((1 - y) * QW, QW))

    for side, d in enumerate((-1, 1)):
        ref = w_far.at[rows_of(turn(x, NX, d), z, c, 96 * side, 96)]
        landed(ref, 4 + side)
        push(ref, ref, 7 + side, sibling)
    for k in range(2):
        for side, d in enumerate((-1, 1)):
            ref = w_far.at[rows_of(x, turn(z, NZ, d), c, 96 * k, 96)]
            landed(ref, 2 * k + side)
            push(ref, ref, 9 + 2 * k + side, sibling)

    await_group(1, 3 - group)
    await_group(2, (group + 2) % 4)

    def far(xx, zz, last=False):
        quarter = (2 * xx + zz) % 4
        multiply(
            2 * (1 - head) + quarter // 2,
            pl.multiple_of((quarter % 2) * 384, 128),
            384,
            w_far,
            pl.multiple_of(quarter * 384, 384),
            last=last,
        )

    own_share.wait()
    landed(w_far.at[rows_of(x, z, 1 - c, 0, 192)], 6)
    far(x, z)
    for side, d in enumerate((-1, 1)):
        landed(w_far.at[rows_of(turn(x, NX, d), z, 1 - c, 96 * side, 96)], 7 + side)
    far(turn(x, NX, 1), z)
    for side, d in enumerate((-1, 1)):
        for k in range(2):
            landed(w_far.at[rows_of(x, turn(z, NZ, d), 1 - c, 96 * k, 96)], 9 + 2 * k + side)
        far(x, turn(z, NZ, d), last=side == 1)

    for copy in (*x_copies, *sent, *y_copies):
        copy.wait_send()


def attend(doc_blocks, queries, keys, values):
    f32, bf16 = jnp.float32, jnp.bfloat16
    smem = pl.BlockSpec(memory_space=pltpu.SMEM)
    width = GROUP * PIECE
    return pl.pallas_call(
        attend_kernel,
        out_shape=jax.ShapeDtypeStruct((NX * NY, PIECE, QW), bf16),
        in_specs=[smem, ANY, ANY, ANY],
        out_specs=VMEM,
        scratch_shapes=[
            pltpu.SMEM((NX * NY,), jnp.int32),
            pltpu.SMEM((NX * NY,), jnp.int32),
            pltpu.VMEM((SEQ + ROWS, HD), bf16),
            pltpu.VMEM((HD, SEQ + ROWS), bf16),
            pltpu.VMEM((NX * NY, PIECE, QW), bf16),
            pltpu.VMEM((NX * NY, HD, width), bf16),
            pltpu.VMEM((HD, width), f32),
            pltpu.VMEM((HD, width), f32),
            pltpu.VMEM((8, width), f32),
            pltpu.VMEM((8, width), f32),
            pltpu.VMEM((8, width), f32),
            pltpu.SemaphoreType.DMA,
            pltpu.SemaphoreType.DMA((SEQ // CHUNK,)),
            pltpu.SemaphoreType.DMA((SEQ // ROWS,)),
        ],
        compiler_params=pltpu.CompilerParams(vmem_limit_bytes=60 << 20),
        name="attend",
    )(doc_blocks, queries, keys, values)


def local(queries, key_vectors, value_vectors, query_taps, key_taps, out_weight, doc_blocks):
    bf16 = jnp.bfloat16
    dma = pltpu.SemaphoreType.DMA
    shape = jax.ShapeDtypeStruct
    model = out_weight.shape[1]
    qx, gk, gv, w_share = pl.pallas_call(
        gather_kernel,
        out_shape=(
            shape((NX, NY, PIECE, QW), bf16),
            shape((NX, NY, NZ, NC, ROWS, HD), bf16),
            shape((NX, NY, NZ, NC, HD, ROWS), bf16),
            shape((192, model // 2), bf16),
        ),
        in_specs=[ANY] * 6,
        out_specs=[ANY] * 4,
        scratch_shapes=[
            pltpu.VMEM((ROWS, 2 * QW), bf16),
            pltpu.VMEM((ROWS, 2 * HD), bf16),
            pltpu.VMEM((ROWS, 2 * HD), bf16),
            pltpu.VMEM((4, 2 * QW), jnp.float32),
            pltpu.VMEM((4, 2 * HD), jnp.float32),
            pltpu.VMEM((16, 2 * QW), bf16),
            pltpu.VMEM((16, 2 * HD), bf16),
            pltpu.VMEM((ROWS, 2 * QW), bf16),
            pltpu.VMEM((ROWS, 2 * HD), bf16),
            pltpu.VMEM((2 * HD, ROWS), bf16),
            dma((5,)), dma((2,)), dma((2,)), dma((2,)), dma((2,)), dma((2,)),
            dma((7,)), dma((7,)), dma, dma, dma,
            dma((4, 36)), dma((4, 36)),
        ],
        compiler_params=pltpu.CompilerParams(
            collective_id=0, has_side_effects=True, vmem_limit_bytes=60 << 20
        ),
        name="gather",
    )(queries, key_vectors, value_vectors, query_taps, key_taps, out_weight)

    attended = attend(
        doc_blocks,
        qx.reshape(NX * NY, PIECE, QW),
        gk.reshape(SEQ, HD),
        gv.reshape(SEQ // ROWS, HD, ROWS),
    )

    return pl.pallas_call(
        project_kernel,
        out_shape=shape((ROWS, model // 2), bf16),
        in_specs=[ANY] * 3,
        out_specs=VMEM,
        scratch_shapes=[
            pltpu.VMEM((4, ROWS, QW), bf16),
            pltpu.VMEM((ROWS, QW), bf16),
            pltpu.VMEM((2 * QW, model // 2), bf16),
            pltpu.VMEM((2 * QW, model // 2), bf16),
            pltpu.VMEM((model // 2 // TILE, ROWS, TILE), jnp.float32),
            dma((3, 2)), dma((3, 2)), dma((2,)), dma((3, 4)), dma((3, 4)),
            dma, dma, dma((13,)), dma((13,)),
        ],
        compiler_params=pltpu.CompilerParams(
            collective_id=1, has_side_effects=True, vmem_limit_bytes=48 << 20
        ),
        name="project",
    )(attended.reshape(NX, NY, PIECE, QW), out_weight, w_share)


def solution(mesh):
    in_specs = (
        P(("inner", "outer"), "head"),
        P(("inner", "outer"), "head"),
        P(("inner", "outer"), "head"),
        P(None, "head"),
        P(None, "head"),
        P("head", None),
        P(),
    )
    out_specs = P(("inner", "outer"), "head")
    return jax.shard_map(local, mesh=mesh, in_specs=in_specs, out_specs=out_specs, check_vma=False)
```

```python
import functools

import jax
import jax.numpy as jnp
from jax import lax
from jax.experimental import pallas as pl
from jax.experimental.pallas import tpu as pltpu
from jax.sharding import PartitionSpec as P

HD = 128
BLOCK = 128
NX, NY, NZ, NC = 4, 2, 4, 2
ROWS = 256
SEQ = 16384
GROUP = 6
PIECE = ROWS // NX
W_PIECES, W_PIECE = 6, 32
QW = GROUP * HD
CHUNK = 1024
LIMIT = 2.0**60
MESH = pl.DeviceIdType.MESH
VMEM = pl.BlockSpec(memory_space=pltpu.VMEM)
ANY = pl.BlockSpec(memory_space=pl.ANY)


def place():
    x = lax.axis_index("inner")
    outer = lax.axis_index("outer")
    return x, outer // (NZ * NC), (outer // NC) % NZ, outer % NC


def at(x, y, z, c):
    return {"inner": x, "outer": y * (NZ * NC) + z * NC + c}


def turn(i, n, d):
    return (i + n + d) % n


def far_rows(x, y, z, c, start, size):
    quarter = (x + z) % 2 + 2 * y
    return pl.ds(pl.multiple_of(quarter * 384 + c * 192 + start, 16), size)


def greet(others):
    barrier = pltpu.get_barrier_semaphore()
    for other in others:
        pl.semaphore_signal(barrier, inc=1, device_id=other, device_id_type=MESH)
    pl.semaphore_wait(barrier, len(others))


def remote(src, dst, send, recv, to):
    return pltpu.make_async_remote_copy(
        src_ref=src, dst_ref=dst, send_sem=send, recv_sem=recv, device_id=to, device_id_type=MESH
    )


def convolve(halo, field, taps, out, width, tile):
    def one(i, carry):
        cols = pl.ds(pl.multiple_of(i * tile, tile), tile)
        wide = jnp.concatenate(
            [halo[:, cols].astype(jnp.float32), field[:, cols].astype(jnp.float32)], axis=0
        )
        total = taps[0:1, cols] * wide[16:]
        for j in range(1, 4):
            total = total + taps[j : j + 1, cols] * wide[16 - j : 16 - j + ROWS]
        out[:, cols] = total.astype(jnp.bfloat16)
        return carry

    lax.fori_loop(0, width // tile, one, 0)


def gather_kernel(
    q_hbm, k_hbm, v_hbm, qt_hbm, kt_hbm, w_hbm, qx_ref, gk_ref, gv_ref, w_ref,
    q_ref, k_ref, v_ref, qt_ref, kt_ref,
    halo_q, halo_k, cq, ck, vt, load_s, halo_s, halo_r, y_s, y_r, own_s, q_s, q_r, q_own, w_s, w_r, send, recv,
):
    x, y, z, c = place()
    head = lax.axis_index("head")
    loads = [
        pltpu.make_async_copy(src, dst, load_s.at[i])
        for i, (src, dst) in enumerate(
            ((k_hbm, k_ref), (v_hbm, v_ref), (kt_hbm, kt_ref), (q_hbm, q_ref), (qt_hbm, qt_ref))
        )
    ]
    for load in loads:
        load.start()
    shard = x * 16 + lax.axis_index("outer")
    after = turn(shard, 64, 1)
    before = turn(shard, 64, -1)
    nxt = {"inner": after // 16, "outer": after % 16}
    prv = {"inner": before // 16, "outer": before % 16}
    across = at(x, 1 - y, z, c)
    opposite = {"head": 1 - head, **across}
    sibling = at(x, y, z, 1 - c)
    steps = {
        "z": (at(x, y, turn(z, NZ, 1), c), at(x, y, turn(z, NZ, -1), c)),
        "x": (at(turn(x, NX, 1), y, z, c), at(turn(x, NX, -1), y, z, c)),
    }
    peers = [
        (dx, dy) for dx in (0, 1, -1, 2) for dy in (0, 1) if (dx, dy) != (0, 0)
    ]
    peer_ids = [at(turn(x, NX, dx), (y + dy) % 2, z, c) for dx, dy in peers]
    greet(
        [nxt, prv, across, opposite, sibling, *steps["z"], *steps["x"]]
        + [d for d, (dx, dy) in zip(peer_ids, peers) if dx == 2 or dy == 1 and dx != 0]
    )

    halos = [
        remote(k_hbm.at[pl.ds(ROWS - 16, 16)], halo_k, halo_s.at[0], halo_r.at[0], nxt),
        remote(q_hbm.at[pl.ds(ROWS - 16, 16)], halo_q, halo_s.at[1], halo_r.at[1], nxt),
    ]
    for copy in halos:
        copy.start()

    mine = pl.ds(pl.multiple_of(y * HD, HD), HD)
    theirs = pl.ds(pl.multiple_of((1 - y) * HD, HD), HD)

    class Part:
        pass

    parts = []
    for index, (full, size, block_y, first, second) in enumerate((
        (gv_ref, HD, y, "x", "z"),
        (gk_ref, ROWS, y, "z", "x"),
        (gv_ref, HD, 1 - y, "x", "z"),
        (gk_ref, ROWS, 1 - y, "z", "x"),
    )):
        part = Part()
        part.index, part.full, part.size, part.y = index, full, size, block_y
        part.first, part.second = steps[first], steps[second]
        part.swap = first == "x"
        part.sends = []
        parts.append(part)
    v_mine, k_mine, v_theirs, k_theirs = parts

    def block(part, da, db, half=None, core=c):
        xx, zz = (turn(x, NX, da), turn(z, NZ, db)) if part.swap else (turn(x, NX, db), turn(z, NZ, da))
        rows = pl.ds(0, part.size) if half is None else pl.ds(half * part.size // 2, part.size // 2)
        return part.full.at[xx, part.y, zz, core, rows]

    def push(part, ref, to, slot, src=None):
        copy = remote(ref if src is None else src, ref, send.at[part.index, slot], recv.at[part.index, slot], to)
        copy.start()
        part.sends.append(copy)

    def landed(part, ref, slot):
        remote(ref, ref, send.at[part.index, slot], recv.at[part.index, slot], across).wait_recv()

    offsets = (0, -1, 1, 2)
    def to_sibling(part, da, db, src=None):
        push(part, block(part, da, db), sibling, 20 + offsets.index(da) * 4 + offsets.index(db), src)

    def second_ring(part, da, src=None):
        k = offsets.index(da)
        for side in range(2):
            push(part, block(part, da, 0), part.second[side], 4 + 2 * k + side, src)
        to_sibling(part, da, 0, src)

    def begin(part, src=None):
        for side in range(2):
            push(part, block(part, 0, 0), part.first[side], side, src)
        second_ring(part, 0, src)

    def ring_step(part):
        landed(part, block(part, -1, 0), 0)
        push(part, block(part, -1, 0, 0), part.first[0], 2)
        landed(part, block(part, 1, 0), 1)
        push(part, block(part, 1, 0, 1), part.first[1], 3)
        second_ring(part, -1)
        second_ring(part, 1)

    def ring_end(part):
        landed(part, block(part, 2, 0, 0), 2)
        landed(part, block(part, 2, 0, 1), 3)
        second_ring(part, 2)

    def pass_on(part, da):
        k = offsets.index(da)
        landed(part, block(part, da, -1), 4 + 2 * k)
        push(part, block(part, da, -1, 0), part.second[0], 12 + 2 * k)
        landed(part, block(part, da, 1), 5 + 2 * k)
        push(part, block(part, da, 1, 1), part.second[1], 13 + 2 * k)
        to_sibling(part, da, -1)
        to_sibling(part, da, 1)

    def finish(part, da):
        k = offsets.index(da)
        landed(part, block(part, da, 2, 0), 12 + 2 * k)
        landed(part, block(part, da, 2, 1), 13 + 2 * k)
        to_sibling(part, da, 2)

    def to_across(part, src):
        copy = remote(src, part.full.at[x, y, z, c], y_s.at[part.index], y_r.at[part.index], across)
        copy.start()
        part.sends.append(copy)

    def from_across(part, source):
        ref = block(part, 0, 0)
        remote(ref, ref, y_s.at[source.index], y_r.at[source.index], across).wait_recv()

    def keep(part, src):
        part.own = pltpu.make_async_copy(src, block(part, 0, 0), own_s.at[part.index])
        part.own.start()

    loads[1].wait()
    vt[...] = v_ref[...].T
    to_across(v_mine, vt.at[theirs])
    begin(v_mine, vt.at[mine])
    keep(v_mine, vt.at[mine])

    loads[0].wait()
    loads[2].wait()
    halos[0].wait_recv()

    @pl.when(shard == 0)
    def _():
        halo_k[...] = jnp.zeros_like(halo_k)

    convolve(halo_k, k_ref, kt_ref, ck, 2 * HD, 128)
    to_across(k_mine, ck.at[:, theirs])
    begin(k_mine, ck.at[:, mine])
    keep(k_mine, ck.at[:, mine])

    half = w_hbm.shape[1] // 2
    w_columns = pl.ds(pl.multiple_of((1 - head) * half, half), half)

    def w_copy(k, origin, to, stage, slot=None):
        dst = w_ref.at[origin, pl.ds(k * W_PIECE, W_PIECE)]
        src = dst if stage else w_hbm.at[far_rows(x, origin, z, c, k * W_PIECE, W_PIECE), w_columns]
        slot = k if slot is None else slot
        return remote(src, dst, w_s.at[stage, slot], w_r.at[stage, slot], to)

    def w_fetches(origin):
        for k in range(W_PIECES):
            yield w_copy(k, origin, opposite, 0)
        yield w_copy(W_PIECES - 1, 1 - origin, opposite, 0, W_PIECES)

    for copy in w_fetches(1 - y):
        copy.start()

    def w_onward(k):
        w_copy(k, y, across, 0).wait_recv()
        w_copy(k, y, across, 1).start()

    from_across(v_theirs, v_mine)
    begin(v_theirs)
    ring_step(v_mine)
    from_across(k_theirs, k_mine)
    begin(k_theirs)
    ring_step(k_mine)

    ring_end(v_mine)
    ring_step(v_theirs)
    w_onward(0)
    loads[3].wait()
    loads[4].wait()
    halos[1].wait_recv()

    @pl.when(shard == 0)
    def _():
        halo_q[...] = jnp.zeros_like(halo_q)

    convolve(halo_q, q_ref, qt_ref, cq, 2 * QW, 128)

    q_copies = []
    for i, ((dx, dy), to) in enumerate(zip(peers, peer_ids)):
        px, py = turn(x, NX, dx), (y + dy) % 2
        piece = cq.at[
            pl.ds(pl.multiple_of(px * PIECE, PIECE), PIECE), pl.ds(pl.multiple_of(py * QW, QW), QW)
        ]
        copy = remote(piece, qx_ref.at[x, y], q_s.at[i], q_r.at[i], to)
        copy.start()
        q_copies.append(copy)
    own_q = pltpu.make_async_copy(
        cq.at[
            pl.ds(pl.multiple_of(x * PIECE, PIECE), PIECE), pl.ds(pl.multiple_of(y * QW, QW), QW)
        ],
        qx_ref.at[x, y],
        q_own,
    )
    own_q.start()

    ring_end(k_mine)
    ring_step(k_theirs)
    ring_end(v_theirs)
    ring_end(k_theirs)
    w_onward(1)
    for i, da in enumerate(offsets):
        for part in parts:
            pass_on(part, da)
        if i % 2:
            w_onward(2 + i // 2)
    for i, da in enumerate(offsets):
        for part in parts:
            finish(part, da)
        if i == 1:
            w_onward(4)

    for part in parts:
        for copy in part.sends:
            copy.wait_send()
        for i, da in enumerate(offsets):
            for j, db in enumerate(offsets):
                landed(part, block(part, da, db, core=1 - c), 20 + 4 * i + j)
    v_mine.own.wait()
    k_mine.own.wait()
    for copy in halos:
        copy.wait_send()
    for i, (dx, dy) in enumerate(peers):
        q_copies[i].wait_send()
        ref = qx_ref.at[turn(x, NX, -dx), (y + dy) % 2]
        remote(ref, ref, q_s.at[i], q_r.at[i], across).wait_recv()
    own_q.wait()
    for copy in w_fetches(1 - y):
        copy.wait_send()
    w_copy(W_PIECES - 1, y, opposite, 0).wait_recv()
    w_copy(W_PIECES - 1, 1 - y, opposite, 0, W_PIECES).wait_recv()
    for k in range(W_PIECES - 1):
        w_copy(k, y, across, 1).wait_send()
        w_copy(k, 1 - y, across, 1).wait_recv()


def find_spans(doc_ref, first_ref, limit_ref):
    x = lax.axis_index("inner")
    outer = lax.axis_index("outer")
    for p in range(NX * NY):
        token = ((p // NY) * 16 + (p % NY) * 8 + outer % 8) * ROWS + x * PIECE
        start = jnp.int32(0)
        first = jnp.int32(0)
        for d in range(doc_ref.shape[0]):
            first = jnp.where(start <= token, start, first)
            start = start + doc_ref[d] * BLOCK
        first_ref[p] = first
        limit_ref[p] = token + PIECE


def attend_kernel(doc_ref, q_ref, gk_ref, gv_ref, o_ref, first_ref, limit_ref, keys, values, q_all, q_t, acc, add, l_s, l_n, m_s, q_sem, k_sem, v_sem):
    def key_load(i):
        rows = pl.ds(pl.multiple_of(i * CHUNK, CHUNK), CHUNK)
        return pltpu.make_async_copy(gk_ref.at[rows], keys.at[rows], k_sem.at[i])

    def value_load(i):
        columns = pl.ds(pl.multiple_of(i * ROWS, ROWS), ROWS)
        return pltpu.make_async_copy(gv_ref.at[i], values.at[:, columns], v_sem.at[i])

    def start_loads(i, carry):
        key_load(i).start()
        for u in range(CHUNK // ROWS):
            value_load(i * (CHUNK // ROWS) + u).start()
        return carry

    q_load = pltpu.make_async_copy(q_ref, q_all, q_sem)
    q_load.start()
    lax.fori_loop(0, SEQ // CHUNK, start_loads, 0)
    find_spans(doc_ref, first_ref, limit_ref)
    keys[SEQ:, :] = jnp.zeros((ROWS, HD), jnp.bfloat16)
    values[:, SEQ:] = jnp.zeros((HD, ROWS), jnp.bfloat16)
    q_load.wait()
    for p in range(NX * NY):
        for h in range(GROUP):
            q_t[p, :, h * PIECE : (h + 1) * PIECE] = q_all[p, :, h * HD : (h + 1) * HD].T

    def wait_loads(i, carry):
        key_load(i).wait()
        for u in range(CHUNK // ROWS):
            value_load(i * (CHUNK // ROWS) + u).wait()
        return carry

    factor = HD**-0.5 * 1.4426950408889634
    width = GROUP * PIECE

    def position(p, carry):
        @pl.when(p % NY == 0)
        def _():
            loads = SEQ // CHUNK // NX
            lax.fori_loop(p // NY * loads, (p // NY + 1) * loads, wait_loads, 0)

        first = first_ref[p]
        limit = limit_ref[p]
        pieces = (limit - first + ROWS - 1) // ROWS
        count = (pieces - 1) // (CHUNK // ROWS)
        rest = pieces - count * (CHUNK // ROWS)

        def scores(start, size):
            return jnp.dot(keys[pl.ds(start, size), :], q_t[p], preferred_element_type=jnp.float32)

        def mix(start, size, weights):
            return jnp.dot(values[:, pl.ds(start, size)], weights, preferred_element_type=jnp.float32)

        def add_up(exps, size):
            return jnp.sum(exps.reshape(size // 8, 8, width), axis=0)

        def tail(size):
            start = pl.multiple_of(first + count * CHUNK, BLOCK)
            s = scores(start, size)
            token = limit - PIECE + lax.rem(
                lax.broadcasted_iota(jnp.int32, (ROWS, width), 1), PIECE
            )
            key = start + size - ROWS + lax.broadcasted_iota(jnp.int32, (ROWS, width), 0)
            edge = jnp.where(key <= token, s[size - ROWS :], -1e30)
            s = edge if size == ROWS else jnp.concatenate([s[: size - ROWS], edge], axis=0)
            top = jnp.max(s, axis=0, keepdims=True)
            exps = jnp.exp2((s - top) * factor)
            l_s[...] = add_up(exps, size)
            m_s[...] = jnp.broadcast_to(top, m_s.shape)
            acc[...] = mix(start, size, exps.astype(jnp.bfloat16))

        for k in range(1, CHUNK // ROWS + 1):
            pl.when(rest == k)(functools.partial(tail, k * ROWS))

        def chunk(i, carry):
            start = pl.multiple_of(first + i * CHUNK, BLOCK)
            exps = jnp.exp2((scores(start, CHUNK) - m_s[0:1, :]) * factor)
            totals = l_s[...] + add_up(exps, CHUNK)
            add[...] = mix(start, CHUNK, exps.astype(jnp.bfloat16))
            l_n[...] = totals
            high = jnp.logical_not(jnp.max(totals) <= LIMIT)

            @pl.when(jnp.logical_not(high))
            def _():
                acc[...] = acc[...] + add[...]
                l_s[...] = l_n[...]

            @pl.when(high)
            def _():
                s = scores(start, CHUNK)
                old = m_s[0:1, :]
                top = jnp.maximum(old, jnp.max(s, axis=0, keepdims=True))
                decay = jnp.exp2((old - top) * factor)
                exps = jnp.exp2((s - top) * factor)
                l_s[...] = l_s[...] * decay + add_up(exps, CHUNK)
                m_s[...] = jnp.broadcast_to(top, m_s.shape)
                acc[...] = acc[...] * decay + mix(start, CHUNK, exps.astype(jnp.bfloat16))

            return carry

        lax.fori_loop(0, count, chunk, 0)
        totals = jnp.sum(l_s[...], axis=0, keepdims=True)
        result = (acc[...] / totals).T
        for h in range(GROUP):
            o_ref[p, :, h * HD : (h + 1) * HD] = result[h * PIECE : (h + 1) * PIECE].astype(
                jnp.bfloat16
            )
        return carry

    lax.fori_loop(0, NX * NY, position, 0)


TILE = 512


def project_kernel(
    o_ref, w_ref, share_ref, out_ref, full, other, w_own, w_far, total,
    x_s, x_r, o_s, y_s, y_r, w_s, own_s, send, recv,
):
    x, y, z, c = place()
    head = lax.axis_index("head")
    group = 2 * head + y
    half = w_ref.shape[1] // 2
    tiles = half // TILE
    sibling = at(x, y, z, 1 - c)
    z_ids = [at(x, y, turn(z, NZ, d), c) for d in (1, -1)]
    x_ids = [at(turn(x, NX, d), y, z, c) for d in (1, -1, 2)]
    across = at(x, 1 - y, z, c)
    y_ids = [across, {"head": 1 - head, **across}, {"head": 1 - head, **at(x, y, z, c)}]

    w_load = pltpu.make_async_copy(
        w_ref.at[:, pl.ds(pl.multiple_of(head * half, half), half)], w_own, w_s
    )
    greet([sibling, *z_ids, *x_ids, *y_ids])

    def piece(xx):
        return pl.ds(pl.multiple_of(xx * PIECE, PIECE), PIECE)

    here = piece(x)
    x_copies = []
    for i, (d, to) in enumerate(zip((1, -1, 2), x_ids)):
        xx = turn(x, NX, d)
        for j, copy in enumerate((
            remote(o_ref.at[xx, 1 - y], other.at[here], x_s.at[i, 0], x_r.at[i, 0], to),
            remote(o_ref.at[xx, y], full.at[group, here], x_s.at[i, 1], x_r.at[i, 1], to),
        )):
            copy.start()
            x_copies.append(copy)
    own_copies = [
        pltpu.make_async_copy(o_ref.at[x, 1 - y], other.at[here], o_s.at[0]),
        pltpu.make_async_copy(o_ref.at[x, y], full.at[group, here], o_s.at[1]),
    ]
    for copy in own_copies:
        copy.start()

    sent = []

    def push(src, dst, slot, to):
        copy = remote(src, dst, send.at[slot], recv.at[slot], to)
        copy.start()
        sent.append(copy)

    def landed(ref, slot):
        remote(ref, ref, send.at[slot], recv.at[slot], sibling).wait_recv()

    for j in range(2):
        for k in range(2):
            rows = far_rows(x, j, z, c, 64 * k, 64)
            push(share_ref.at[j, pl.ds(64 * k, 64)], w_far.at[rows], 2 * j + k, z_ids[j])
        rows = far_rows(x, j, z, c, 128, 64)
        push(share_ref.at[j, pl.ds(128, 64)], w_far.at[rows], 4 + j, x_ids[j])
    own_shares = []
    for j in range(2):
        mine = w_far.at[far_rows(x, j, z, c, 0, 192)]
        push(share_ref.at[j], mine, 6 + j, sibling)
        own_shares.append(pltpu.make_async_copy(share_ref.at[j], mine, own_s.at[j]))
        own_shares[j].start()
    w_load.start()

    y_copies = []

    def onward(i, xx):
        rows = piece(xx)
        for r, (src, to) in enumerate(
            zip((other.at[rows], other.at[rows], full.at[group, rows]), y_ids)
        ):
            copy = remote(src, full.at[group, rows], y_s.at[r, i], y_r.at[r, i], to)
            copy.start()
            y_copies.append(copy)

    for copy in own_copies:
        copy.wait()
    onward(3, x)
    for i, d in enumerate((1, -1, 2)):
        xx = turn(x, NX, -d)
        rows = piece(xx)
        remote(other.at[rows], other.at[rows], x_s.at[i, 0], x_r.at[i, 0], sibling).wait_recv()
        ref = full.at[group, rows]
        remote(ref, ref, x_s.at[i, 1], x_r.at[i, 1], sibling).wait_recv()
        onward(i, xx)

    def multiply(g, column, depth, w, row, first=False, last=False):
        def one(t, carry):
            cols = pl.ds(pl.multiple_of(t * TILE, TILE), TILE)
            value = jnp.dot(
                full[g, :, pl.ds(column, depth)], w[pl.ds(row, depth), cols], preferred_element_type=jnp.float32
            )
            if not first:
                value = value + total[t]
            if last:
                out_ref[:, cols] = value.astype(jnp.bfloat16)
            else:
                total[t] = value
            return carry

        lax.fori_loop(0, tiles, one, 0)

    w_load.wait()
    multiply(group, 0, QW, w_own, pl.multiple_of(y * QW, QW), first=True)

    def await_group(r, g):
        for i, d in enumerate((1, -1, 2, 0)):
            ref = full.at[g, piece(turn(x, NX, -d))]
            remote(ref, ref, y_s.at[r, i], y_r.at[r, i], sibling).wait_recv()

    await_group(0, group + 1 - 2 * y)
    multiply(group + 1 - 2 * y, 0, QW, w_own, pl.multiple_of((1 - y) * QW, QW))

    def arrivals(core):
        for j, d in enumerate((-1, 1)):
            yield 4 + j, 12 + j, w_far.at[far_rows(turn(x, NX, d), j, z, core, 128, 64)]
        for k in range(2):
            for j, d in enumerate((-1, 1)):
                yield 2 * j + k, 8 + 2 * j + k, w_far.at[far_rows(x, j, turn(z, NZ, d), core, 64 * k, 64)]

    for slot, onto, ref in arrivals(c):
        landed(ref, slot)
        push(ref, ref, onto, sibling)

    await_group(1, 3 - group)
    await_group(2, (group + 2) % 4)

    def far(parity, j, last=False):
        quarter = parity + 2 * j
        multiply(
            2 * (1 - head) + j,
            pl.multiple_of(parity * 384, 128),
            384,
            w_far,
            pl.multiple_of(quarter * 384, 384),
            last=last,
        )

    parity = (x + z) % 2
    for j in range(2):
        own_shares[j].wait()
        landed(w_far.at[far_rows(x, j, z, 1 - c, 0, 192)], 6 + j)
        far(parity, j)
    for slot, onto, ref in arrivals(1 - c):
        landed(ref, onto)
    for j in range(2):
        far(1 - parity, j, last=j == 1)

    for copy in (*x_copies, *sent, *y_copies):
        copy.wait_send()


def attend(doc_blocks, queries, keys, values):
    f32, bf16 = jnp.float32, jnp.bfloat16
    smem = pl.BlockSpec(memory_space=pltpu.SMEM)
    width = GROUP * PIECE
    return pl.pallas_call(
        attend_kernel,
        out_shape=jax.ShapeDtypeStruct((NX * NY, PIECE, QW), bf16),
        in_specs=[smem, ANY, ANY, ANY],
        out_specs=VMEM,
        scratch_shapes=[
            pltpu.SMEM((NX * NY,), jnp.int32),
            pltpu.SMEM((NX * NY,), jnp.int32),
            pltpu.VMEM((SEQ + ROWS, HD), bf16),
            pltpu.VMEM((HD, SEQ + ROWS), bf16),
            pltpu.VMEM((NX * NY, PIECE, QW), bf16),
            pltpu.VMEM((NX * NY, HD, width), bf16),
            pltpu.VMEM((HD, width), f32),
            pltpu.VMEM((HD, width), f32),
            pltpu.VMEM((8, width), f32),
            pltpu.VMEM((8, width), f32),
            pltpu.VMEM((8, width), f32),
            pltpu.SemaphoreType.DMA,
            pltpu.SemaphoreType.DMA((SEQ // CHUNK,)),
            pltpu.SemaphoreType.DMA((SEQ // ROWS,)),
        ],
        compiler_params=pltpu.CompilerParams(vmem_limit_bytes=60 << 20),
        name="attend",
    )(doc_blocks, queries, keys, values)


def local(queries, key_vectors, value_vectors, query_taps, key_taps, out_weight, doc_blocks):
    bf16 = jnp.bfloat16
    dma = pltpu.SemaphoreType.DMA
    shape = jax.ShapeDtypeStruct
    model = out_weight.shape[1]
    qx, gk, gv, w_share = pl.pallas_call(
        gather_kernel,
        out_shape=(
            shape((NX, NY, PIECE, QW), bf16),
            shape((NX, NY, NZ, NC, ROWS, HD), bf16),
            shape((NX, NY, NZ, NC, HD, ROWS), bf16),
            shape((NY, W_PIECES * W_PIECE, model // 2), bf16),
        ),
        in_specs=[ANY] * 6,
        out_specs=[ANY] * 4,
        scratch_shapes=[
            pltpu.VMEM((ROWS, 2 * QW), bf16),
            pltpu.VMEM((ROWS, 2 * HD), bf16),
            pltpu.VMEM((ROWS, 2 * HD), bf16),
            pltpu.VMEM((4, 2 * QW), jnp.float32),
            pltpu.VMEM((4, 2 * HD), jnp.float32),
            pltpu.VMEM((16, 2 * QW), bf16),
            pltpu.VMEM((16, 2 * HD), bf16),
            pltpu.VMEM((ROWS, 2 * QW), bf16),
            pltpu.VMEM((ROWS, 2 * HD), bf16),
            pltpu.VMEM((2 * HD, ROWS), bf16),
            dma((5,)), dma((2,)), dma((2,)), dma((2,)), dma((2,)), dma((2,)),
            dma((7,)), dma((7,)), dma, dma((2, W_PIECES + 1)), dma((2, W_PIECES + 1)),
            dma((4, 36)), dma((4, 36)),
        ],
        compiler_params=pltpu.CompilerParams(
            collective_id=0, has_side_effects=True, vmem_limit_bytes=60 << 20
        ),
        name="gather",
    )(queries, key_vectors, value_vectors, query_taps, key_taps, out_weight)

    attended = attend(
        doc_blocks,
        qx.reshape(NX * NY, PIECE, QW),
        gk.reshape(SEQ, HD),
        gv.reshape(SEQ // ROWS, HD, ROWS),
    )

    return pl.pallas_call(
        project_kernel,
        out_shape=shape((ROWS, model // 2), bf16),
        in_specs=[ANY] * 3,
        out_specs=VMEM,
        scratch_shapes=[
            pltpu.VMEM((4, ROWS, QW), bf16),
            pltpu.VMEM((ROWS, QW), bf16),
            pltpu.VMEM((2 * QW, model // 2), bf16),
            pltpu.VMEM((2 * QW, model // 2), bf16),
            pltpu.VMEM((model // 2 // TILE, ROWS, TILE), jnp.float32),
            dma((3, 2)), dma((3, 2)), dma((2,)), dma((3, 4)), dma((3, 4)),
            dma, dma((2,)), dma((14,)), dma((14,)),
        ],
        compiler_params=pltpu.CompilerParams(
            collective_id=1, has_side_effects=True, vmem_limit_bytes=48 << 20
        ),
        name="project",
    )(attended.reshape(NX, NY, PIECE, QW), out_weight, w_share)


def solution(mesh):
    in_specs = (
        P(("inner", "outer"), "head"),
        P(("inner", "outer"), "head"),
        P(("inner", "outer"), "head"),
        P(None, "head"),
        P(None, "head"),
        P("head", None),
        P(),
    )
    out_specs = P(("inner", "outer"), "head")
    return jax.shard_map(local, mesh=mesh, in_specs=in_specs, out_specs=out_specs, check_vma=False)
```

```python
import functools

import jax
import jax.numpy as jnp
from jax import lax
from jax.experimental import pallas as pl
from jax.experimental.pallas import tpu as pltpu
from jax.sharding import PartitionSpec as P

HD = 128
BLOCK = 128
NX, NY, NZ, NC = 4, 2, 4, 2
ROWS = 256
SEQ = 16384
GROUP = 6
PIECE = ROWS // NX
W_PIECES, W_PIECE = 6, 32
QW = GROUP * HD
CHUNK = 1024
LIMIT = 2.0**60
SPARE = 24
MESH = pl.DeviceIdType.MESH
VMEM = pl.BlockSpec(memory_space=pltpu.VMEM)
ANY = pl.BlockSpec(memory_space=pl.ANY)


def place():
    x = lax.axis_index("inner")
    outer = lax.axis_index("outer")
    return x, outer // (NZ * NC), (outer // NC) % NZ, outer % NC


def at(x, y, z, c):
    return {"inner": x, "outer": y * (NZ * NC) + z * NC + c}


def turn(i, n, d):
    return (i + n + d) % n


def far_rows(x, y, z, c, start, size):
    quarter = (x + z) % 2 + 2 * y
    return pl.ds(pl.multiple_of(quarter * 384 + c * 192 + start, 16), size)


def greet(others):
    barrier = pltpu.get_barrier_semaphore()
    for other in others:
        pl.semaphore_signal(barrier, inc=1, device_id=other, device_id_type=MESH)
    pl.semaphore_wait(barrier, len(others))


def remote(src, dst, send, recv, to):
    return pltpu.make_async_remote_copy(
        src_ref=src, dst_ref=dst, send_sem=send, recv_sem=recv, device_id=to, device_id_type=MESH
    )


def convolve(halo, field, taps, out, width, tile):
    def one(i, carry):
        cols = pl.ds(pl.multiple_of(i * tile, tile), tile)
        wide = jnp.concatenate(
            [halo[:, cols].astype(jnp.float32), field[:, cols].astype(jnp.float32)], axis=0
        )
        total = taps[0:1, cols] * wide[16:]
        for j in range(1, 4):
            total = total + taps[j : j + 1, cols] * wide[16 - j : 16 - j + ROWS]
        out[:, cols] = total.astype(jnp.bfloat16)
        return carry

    lax.fori_loop(0, width // tile, one, 0)


def gather_kernel(
    q_hbm, k_hbm, v_hbm, qt_hbm, kt_hbm, w_hbm, qx_ref, gk_ref, gv_ref, w_ref,
    q_ref, k_ref, v_ref, qt_ref, kt_ref,
    halo_q, halo_k, cq, ck, vt, load_s, halo_s, halo_r, y_s, y_r, own_s, q_s, q_r, q_own, w_s, w_r, send, recv,
):
    x, y, z, c = place()
    head = lax.axis_index("head")
    loads = [
        pltpu.make_async_copy(src, dst, load_s.at[i])
        for i, (src, dst) in enumerate(
            ((k_hbm, k_ref), (v_hbm, v_ref), (kt_hbm, kt_ref), (q_hbm, q_ref), (qt_hbm, qt_ref))
        )
    ]
    for load in loads:
        load.start()
    shard = x * 16 + lax.axis_index("outer")
    after = turn(shard, 64, 1)
    before = turn(shard, 64, -1)
    nxt = {"inner": after // 16, "outer": after % 16}
    prv = {"inner": before // 16, "outer": before % 16}
    across = at(x, 1 - y, z, c)
    opposite = {"head": 1 - head, **across}
    sibling = at(x, y, z, 1 - c)
    steps = {
        "z": (at(x, y, turn(z, NZ, 1), c), at(x, y, turn(z, NZ, -1), c)),
        "x": (at(turn(x, NX, 1), y, z, c), at(turn(x, NX, -1), y, z, c)),
    }
    peers = [
        (dx, dy) for dx in (0, 1, -1, 2) for dy in (0, 1) if (dx, dy) != (0, 0)
    ]
    peer_ids = [at(turn(x, NX, dx), (y + dy) % 2, z, c) for dx, dy in peers]
    greet(
        [nxt, prv, across, opposite, sibling, *steps["z"], *steps["x"]]
        + [d for d, (dx, dy) in zip(peer_ids, peers) if dx == 2 or dy == 1 and dx != 0]
    )

    halos = [
        remote(k_hbm.at[pl.ds(ROWS - 16, 16)], halo_k, halo_s.at[0], halo_r.at[0], nxt),
        remote(q_hbm.at[pl.ds(ROWS - 16, 16)], halo_q, halo_s.at[1], halo_r.at[1], nxt),
    ]
    for copy in halos:
        copy.start()

    mine = pl.ds(pl.multiple_of(y * HD, HD), HD)
    theirs = pl.ds(pl.multiple_of((1 - y) * HD, HD), HD)

    class Part:
        pass

    parts = []
    for index, (full, size, block_y, first, second) in enumerate((
        (gv_ref, HD, y, "x", "z"),
        (gk_ref, ROWS, y, "z", "x"),
        (gv_ref, HD, 1 - y, "x", "z"),
        (gk_ref, ROWS, 1 - y, "z", "x"),
    )):
        part = Part()
        part.index, part.full, part.size, part.y = index, full, size, block_y
        part.first, part.second = steps[first], steps[second]
        part.swap = first == "x"
        part.sends = []
        parts.append(part)
    v_mine, k_mine, v_theirs, k_theirs = parts

    def block(part, da, db, half=None, core=c):
        xx, zz = (turn(x, NX, da), turn(z, NZ, db)) if part.swap else (turn(x, NX, db), turn(z, NZ, da))
        rows = pl.ds(0, part.size) if half is None else pl.ds(half * part.size // 2, part.size // 2)
        return part.full.at[xx, part.y, zz, core, rows]

    def push(part, ref, to, slot, src=None):
        copy = remote(ref if src is None else src, ref, send.at[part.index, slot], recv.at[part.index, slot], to)
        copy.start()
        part.sends.append(copy)

    def landed(part, ref, slot):
        remote(ref, ref, send.at[part.index, slot], recv.at[part.index, slot], across).wait_recv()

    offsets = (0, -1, 1, 2)
    def to_sibling(part, da, db, src=None):
        push(part, block(part, da, db), sibling, 20 + offsets.index(da) * 4 + offsets.index(db), src)

    def second_ring(part, da, src=None):
        k = offsets.index(da)
        for side in range(2):
            push(part, block(part, da, 0), part.second[side], 4 + 2 * k + side, src)
        to_sibling(part, da, 0, src)

    def begin(part, src=None):
        for side in range(2):
            push(part, block(part, 0, 0), part.first[side], side, src)
        second_ring(part, 0, src)

    def ring_step(part):
        landed(part, block(part, -1, 0), 0)
        push(part, block(part, -1, 0, 0), part.first[0], 2)
        landed(part, block(part, 1, 0), 1)
        push(part, block(part, 1, 0, 1), part.first[1], 3)
        second_ring(part, -1)
        second_ring(part, 1)

    def ring_end(part):
        landed(part, block(part, 2, 0, 0), 2)
        landed(part, block(part, 2, 0, 1), 3)
        second_ring(part, 2)

    def pass_on(part, da):
        k = offsets.index(da)
        landed(part, block(part, da, -1), 4 + 2 * k)
        push(part, block(part, da, -1, 0), part.second[0], 12 + 2 * k)
        landed(part, block(part, da, 1), 5 + 2 * k)
        push(part, block(part, da, 1, 1), part.second[1], 13 + 2 * k)
        to_sibling(part, da, -1)
        to_sibling(part, da, 1)

    def finish(part, da):
        k = offsets.index(da)
        landed(part, block(part, da, 2, 0), 12 + 2 * k)
        landed(part, block(part, da, 2, 1), 13 + 2 * k)
        to_sibling(part, da, 2)

    def to_across(part, src):
        copy = remote(src, part.full.at[x, y, z, c], y_s.at[part.index], y_r.at[part.index], across)
        copy.start()
        part.sends.append(copy)

    def from_across(part, source):
        ref = block(part, 0, 0)
        remote(ref, ref, y_s.at[source.index], y_r.at[source.index], across).wait_recv()

    def keep(part, src):
        part.own = pltpu.make_async_copy(src, block(part, 0, 0), own_s.at[part.index])
        part.own.start()

    loads[1].wait()
    vt[...] = v_ref[...].T
    to_across(v_mine, vt.at[theirs])
    begin(v_mine, vt.at[mine])
    keep(v_mine, vt.at[mine])

    loads[0].wait()
    loads[2].wait()
    halos[0].wait_recv()

    @pl.when(shard == 0)
    def _():
        halo_k[...] = jnp.zeros_like(halo_k)

    convolve(halo_k, k_ref, kt_ref, ck, 2 * HD, 128)
    to_across(k_mine, ck.at[:, theirs])
    begin(k_mine, ck.at[:, mine])
    keep(k_mine, ck.at[:, mine])

    half = w_hbm.shape[1] // 2
    w_columns = pl.ds(pl.multiple_of((1 - head) * half, half), half)

    def w_copy(k, origin, to, stage, slot=None):
        dst = w_ref.at[origin, pl.ds(k * W_PIECE, W_PIECE)]
        src = dst if stage else w_hbm.at[far_rows(x, origin, z, c, k * W_PIECE, W_PIECE), w_columns]
        slot = k if slot is None else slot
        return remote(src, dst, w_s.at[stage, slot], w_r.at[stage, slot], to)

    def w_fetches(origin):
        for k in range(W_PIECES):
            yield w_copy(k, origin, opposite, 0)
        yield w_copy(W_PIECES - 1, 1 - origin, opposite, 0, W_PIECES)

    for copy in w_fetches(1 - y):
        copy.start()

    def w_onward(k):
        w_copy(k, y, across, 0).wait_recv()
        w_copy(k, y, across, 1).start()

    from_across(v_theirs, v_mine)
    begin(v_theirs)
    ring_step(v_mine)
    from_across(k_theirs, k_mine)
    begin(k_theirs)
    ring_step(k_mine)

    ring_end(v_mine)
    ring_step(v_theirs)
    w_onward(0)
    loads[3].wait()
    loads[4].wait()
    halos[1].wait_recv()

    @pl.when(shard == 0)
    def _():
        halo_q[...] = jnp.zeros_like(halo_q)

    convolve(halo_q, q_ref, qt_ref, cq, 2 * QW, 128)

    q_copies = []
    for i, ((dx, dy), to) in enumerate(zip(peers, peer_ids)):
        px, py = turn(x, NX, dx), (y + dy) % 2
        piece = cq.at[
            pl.ds(pl.multiple_of(px * PIECE, PIECE), PIECE), pl.ds(pl.multiple_of(py * QW, QW), QW)
        ]
        copy = remote(piece, qx_ref.at[x, y], q_s.at[i], q_r.at[i], to)
        copy.start()
        q_copies.append(copy)
    own_q = pltpu.make_async_copy(
        cq.at[
            pl.ds(pl.multiple_of(x * PIECE, PIECE), PIECE), pl.ds(pl.multiple_of(y * QW, QW), QW)
        ],
        qx_ref.at[x, y],
        q_own,
    )
    own_q.start()

    ring_end(k_mine)
    ring_step(k_theirs)
    ring_end(v_theirs)
    ring_end(k_theirs)
    w_onward(1)
    for i, da in enumerate(offsets):
        for part in parts:
            pass_on(part, da)
        if i % 2:
            w_onward(2 + i // 2)
    for i, da in enumerate(offsets):
        for part in parts:
            finish(part, da)
        if i == 1:
            w_onward(4)

    for part in parts:
        for copy in part.sends:
            copy.wait_send()
        for i, da in enumerate(offsets):
            for j, db in enumerate(offsets):
                landed(part, block(part, da, db, core=1 - c), 20 + 4 * i + j)
    v_mine.own.wait()
    k_mine.own.wait()
    for copy in halos:
        copy.wait_send()
    for i, (dx, dy) in enumerate(peers):
        q_copies[i].wait_send()
        ref = qx_ref.at[turn(x, NX, -dx), (y + dy) % 2]
        remote(ref, ref, q_s.at[i], q_r.at[i], across).wait_recv()
    own_q.wait()
    for copy in w_fetches(1 - y):
        copy.wait_send()
    w_copy(W_PIECES - 1, y, opposite, 0).wait_recv()
    w_copy(W_PIECES - 1, 1 - y, opposite, 0, W_PIECES).wait_recv()
    for k in range(W_PIECES - 1):
        w_copy(k, y, across, 1).wait_send()
        w_copy(k, 1 - y, across, 1).wait_recv()


def find_spans(doc_ref, first_ref, limit_ref):
    x = lax.axis_index("inner")
    outer = lax.axis_index("outer")
    for p in range(NX * NY):
        token = ((p // NY) * 16 + (p % NY) * 8 + outer % 8) * ROWS + x * PIECE
        start = jnp.int32(0)
        first = jnp.int32(0)
        for d in range(doc_ref.shape[0]):
            first = jnp.where(start <= token, start, first)
            start = start + doc_ref[d] * BLOCK
        first_ref[p] = first
        limit_ref[p] = token + PIECE


def attend_kernel(doc_ref, q_ref, gk_ref, gv_ref, o_ref, first_ref, limit_ref, keys, values, q_all, o_all, q_t, acc, add, l_s, l_n, m_s, q_sem, o_sem, k_sem, v_sem):
    def key_load(i):
        rows = pl.ds(pl.multiple_of(i * CHUNK, CHUNK), CHUNK)
        return pltpu.make_async_copy(gk_ref.at[rows], keys.at[rows], k_sem.at[i])

    def value_load(i):
        columns = pl.ds(pl.multiple_of(i * ROWS, ROWS), ROWS)
        return pltpu.make_async_copy(gv_ref.at[i], values.at[:, columns], v_sem.at[i])

    def start_loads(i, carry):
        key_load(i).start()
        for u in range(CHUNK // ROWS):
            value_load(i * (CHUNK // ROWS) + u).start()
        return carry

    q_load = pltpu.make_async_copy(q_ref, q_all, q_sem)
    q_load.start()
    lax.fori_loop(0, SEQ // CHUNK, start_loads, 0)
    find_spans(doc_ref, first_ref, limit_ref)
    keys[SEQ:, :] = jnp.zeros((ROWS, HD), jnp.bfloat16)
    values[:, SEQ:] = jnp.zeros((HD, ROWS), jnp.bfloat16)
    q_load.wait()
    for p in range(NX * NY):
        for h in range(GROUP):
            q_t[p, :, h * PIECE : (h + 1) * PIECE] = q_all[p, :, h * HD : (h + 1) * HD].T

    def wait_loads(i, carry):
        key_load(i).wait()
        for u in range(CHUNK // ROWS):
            value_load(i * (CHUNK // ROWS) + u).wait()
        return carry

    factor = HD**-0.5 * 1.4426950408889634
    width = GROUP * PIECE

    def store(p):
        return pltpu.make_async_copy(o_all.at[p], o_ref.at[p], o_sem.at[p])

    def position(p, carry):
        @pl.when(p % NY == 0)
        def _():
            loads = SEQ // CHUNK // NX
            lax.fori_loop(p // NY * loads, (p // NY + 1) * loads, wait_loads, 0)

        first = first_ref[p]
        limit = limit_ref[p]
        pieces = (limit - first + ROWS - 1) // ROWS
        count = (pieces - 1) // (CHUNK // ROWS)
        rest = pieces - count * (CHUNK // ROWS)

        def scores(start, size):
            return jnp.dot(keys[pl.ds(start, size), :], q_t[p], preferred_element_type=jnp.float32)

        def mix(start, size, weights):
            return jnp.dot(values[:, pl.ds(start, size)], weights, preferred_element_type=jnp.float32)

        def add_up(exps, size):
            return jnp.sum(exps.reshape(size // 8, 8, width), axis=0)

        def tail(size):
            start = pl.multiple_of(first + count * CHUNK, BLOCK)
            s = scores(start, size)
            token = limit - PIECE + lax.rem(
                lax.broadcasted_iota(jnp.int32, (ROWS, width), 1), PIECE
            )
            key = start + size - ROWS + lax.broadcasted_iota(jnp.int32, (ROWS, width), 0)
            edge = jnp.where(key <= token, s[size - ROWS :], -1e30)
            s = edge if size == ROWS else jnp.concatenate([s[: size - ROWS], edge], axis=0)
            top = jnp.max(s, axis=0, keepdims=True)
            exps = jnp.exp2((s - top) * factor)
            l_s[...] = add_up(exps, size)
            m_s[...] = jnp.broadcast_to(top, m_s.shape)
            acc[...] = mix(start, size, exps.astype(jnp.bfloat16))

        for k in range(1, CHUNK // ROWS + 1):
            pl.when(rest == k)(functools.partial(tail, k * ROWS))

        def chunk(start, size):
            exps = jnp.exp2((scores(start, size) - m_s[0:1, :]) * factor)
            totals = l_s[...] + add_up(exps, size)
            add[...] = mix(start, size, exps.astype(jnp.bfloat16))
            l_n[...] = totals
            high = jnp.logical_not(jnp.max(totals) <= LIMIT)

            @pl.when(jnp.logical_not(high))
            def _():
                acc[...] = acc[...] + add[...]
                l_s[...] = l_n[...]

            @pl.when(high)
            def _():
                def redo(i, carry):
                    at_rows = pl.multiple_of(start + i * CHUNK, BLOCK)
                    s = scores(at_rows, CHUNK)
                    old = m_s[0:1, :]
                    top = jnp.maximum(old, jnp.max(s, axis=0, keepdims=True))
                    decay = jnp.exp2((old - top) * factor)
                    exps = jnp.exp2((s - top) * factor)
                    l_s[...] = l_s[...] * decay + add_up(exps, CHUNK)
                    m_s[...] = jnp.broadcast_to(top, m_s.shape)
                    acc[...] = acc[...] * decay + mix(at_rows, CHUNK, exps.astype(jnp.bfloat16))
                    return carry

                lax.fori_loop(0, size // CHUNK, redo, 0)

        def double(i, carry):
            chunk(pl.multiple_of(first + i * 2 * CHUNK, BLOCK), 2 * CHUNK)
            return carry

        lax.fori_loop(0, count // 2, double, 0)

        @pl.when(count % 2 == 1)
        def _():
            chunk(pl.multiple_of(first + (count - 1) * CHUNK, BLOCK), CHUNK)

        totals = jnp.sum(l_s[...], axis=0, keepdims=True)
        result = (acc[...] / totals).T
        for h in range(GROUP):
            o_all[p, :, h * HD : (h + 1) * HD] = result[h * PIECE : (h + 1) * PIECE].astype(
                jnp.bfloat16
            )
        store(p).start()
        return carry

    lax.fori_loop(0, NX * NY, position, 0)
    for p in range(NX * NY):
        store(p).wait()


TILE = 512


def project_kernel(
    o_ref, w_ref, share_ref, out_ref, full, other, w_own, w_far, total,
    x_s, x_r, o_s, y_s, y_r, w_s, own_s, send, recv,
):
    x, y, z, c = place()
    head = lax.axis_index("head")
    group = 2 * head + y
    half = w_ref.shape[1] // 2
    tiles = half // TILE
    sibling = at(x, y, z, 1 - c)
    z_ids = [at(x, y, turn(z, NZ, d), c) for d in (1, -1)]
    x_ids = [at(turn(x, NX, d), y, z, c) for d in (1, -1, 2)]
    across = at(x, 1 - y, z, c)
    y_ids = [across, {"head": 1 - head, **across}, {"head": 1 - head, **at(x, y, z, c)}]

    w_load = pltpu.make_async_copy(
        w_ref.at[:, pl.ds(pl.multiple_of(head * half, half), half)], w_own, w_s
    )
    greet([sibling, *z_ids, *x_ids, *y_ids])

    def piece(xx):
        return pl.ds(pl.multiple_of(xx * PIECE, PIECE), PIECE)

    here = piece(x)
    x_copies = []
    for i, (d, to) in enumerate(zip((1, -1, 2), x_ids)):
        xx = turn(x, NX, d)
        for j, copy in enumerate((
            remote(o_ref.at[xx * NY + 1 - y], other.at[here], x_s.at[i, 0], x_r.at[i, 0], to),
            remote(o_ref.at[xx * NY + y], full.at[group, here], x_s.at[i, 1], x_r.at[i, 1], to),
        )):
            copy.start()
            x_copies.append(copy)
    own_copies = [
        pltpu.make_async_copy(o_ref.at[x * NY + 1 - y], other.at[here], o_s.at[0]),
        pltpu.make_async_copy(o_ref.at[x * NY + y], full.at[group, here], o_s.at[1]),
    ]
    for copy in own_copies:
        copy.start()

    sent = []

    def push(src, dst, slot, to):
        copy = remote(src, dst, send.at[slot], recv.at[slot], to)
        copy.start()
        sent.append(copy)

    def landed(ref, slot):
        remote(ref, ref, send.at[slot], recv.at[slot], sibling).wait_recv()

    for j in range(2):
        for k in range(2):
            rows = far_rows(x, j, z, c, 64 * k, 64)
            push(share_ref.at[j, pl.ds(64 * k, 64)], w_far.at[rows], 2 * j + k, z_ids[j])
        rows = far_rows(x, j, z, c, 128, 64)
        push(share_ref.at[j, pl.ds(128, 64)], w_far.at[rows], 4 + j, x_ids[j])
    own_shares = []
    for j in range(2):
        mine = w_far.at[far_rows(x, j, z, c, 0, 192)]
        push(share_ref.at[j], mine, 6 + j, sibling)
        own_shares.append(pltpu.make_async_copy(share_ref.at[j], mine, own_s.at[j]))
        own_shares[j].start()
    w_load.start()

    y_copies = []

    def onward(i, xx):
        rows = piece(xx)
        for r, (src, to) in enumerate(
            zip((other.at[rows], other.at[rows], full.at[group, rows]), y_ids)
        ):
            copy = remote(src, full.at[group, rows], y_s.at[r, i], y_r.at[r, i], to)
            copy.start()
            y_copies.append(copy)

    for copy in own_copies:
        copy.wait()
    onward(3, x)
    for i, d in enumerate((1, -1, 2)):
        xx = turn(x, NX, -d)
        rows = piece(xx)
        remote(other.at[rows], other.at[rows], x_s.at[i, 0], x_r.at[i, 0], sibling).wait_recv()
        ref = full.at[group, rows]
        remote(ref, ref, x_s.at[i, 1], x_r.at[i, 1], sibling).wait_recv()
        onward(i, xx)

    def multiply(g, column, depth, w, row, first=False, last=False):
        def one(t, carry):
            cols = pl.ds(pl.multiple_of(t * TILE, TILE), TILE)
            value = jnp.dot(
                full[g, :, pl.ds(column, depth)], w[pl.ds(row, depth), cols], preferred_element_type=jnp.float32
            )
            if not first:
                value = value + total[t]
            if last:
                out_ref[:, cols] = value.astype(jnp.bfloat16)
            else:
                total[t] = value
            return carry

        lax.fori_loop(0, tiles, one, 0)

    w_load.wait()
    multiply(group, 0, QW, w_own, pl.multiple_of(y * QW, QW), first=True)

    def await_group(r, g):
        for i, d in enumerate((1, -1, 2, 0)):
            ref = full.at[g, piece(turn(x, NX, -d))]
            remote(ref, ref, y_s.at[r, i], y_r.at[r, i], sibling).wait_recv()

    await_group(0, group + 1 - 2 * y)
    multiply(group + 1 - 2 * y, 0, QW, w_own, pl.multiple_of((1 - y) * QW, QW))

    def arrivals(core):
        for j, d in enumerate((-1, 1)):
            yield 4 + j, 12 + j, w_far.at[far_rows(turn(x, NX, d), j, z, core, 128, 64)]
        for k in range(2):
            for j, d in enumerate((-1, 1)):
                yield 2 * j + k, 8 + 2 * j + k, w_far.at[far_rows(x, j, turn(z, NZ, d), core, 64 * k, 64)]

    for slot, onto, ref in arrivals(c):
        landed(ref, slot)
        push(ref, ref, onto, sibling)

    await_group(1, 3 - group)
    await_group(2, (group + 2) % 4)

    def far(parity, j, last=False):
        quarter = parity + 2 * j
        multiply(
            2 * (1 - head) + j,
            pl.multiple_of(parity * 384, 128),
            384,
            w_far,
            pl.multiple_of(quarter * 384, 384),
            last=last,
        )

    parity = (x + z) % 2
    for j in range(2):
        own_shares[j].wait()
        landed(w_far.at[far_rows(x, j, z, 1 - c, 0, 192)], 6 + j)
        far(parity, j)
    for slot, onto, ref in arrivals(1 - c):
        landed(ref, onto)
    for j in range(2):
        far(1 - parity, j, last=j == 1)

    for copy in (*x_copies, *sent, *y_copies):
        copy.wait_send()


def attend(doc_blocks, queries, keys, values):
    f32, bf16 = jnp.float32, jnp.bfloat16
    smem = pl.BlockSpec(memory_space=pltpu.SMEM)
    width = GROUP * PIECE
    return pl.pallas_call(
        attend_kernel,
        out_shape=jax.ShapeDtypeStruct((SPARE * NX * NY, PIECE, QW), bf16),
        in_specs=[smem, ANY, ANY, ANY],
        out_specs=ANY,
        scratch_shapes=[
            pltpu.SMEM((NX * NY,), jnp.int32),
            pltpu.SMEM((NX * NY,), jnp.int32),
            pltpu.VMEM((SEQ + ROWS, HD), bf16),
            pltpu.VMEM((HD, SEQ + ROWS), bf16),
            pltpu.VMEM((NX * NY, PIECE, QW), bf16),
            pltpu.VMEM((NX * NY, PIECE, QW), bf16),
            pltpu.VMEM((NX * NY, HD, width), bf16),
            pltpu.VMEM((HD, width), f32),
            pltpu.VMEM((HD, width), f32),
            pltpu.VMEM((8, width), f32),
            pltpu.VMEM((8, width), f32),
            pltpu.VMEM((8, width), f32),
            pltpu.SemaphoreType.DMA,
            pltpu.SemaphoreType.DMA((NX * NY,)),
            pltpu.SemaphoreType.DMA((SEQ // CHUNK,)),
            pltpu.SemaphoreType.DMA((SEQ // ROWS,)),
        ],
        compiler_params=pltpu.CompilerParams(vmem_limit_bytes=60 << 20),
        name="attend",
    )(doc_blocks, queries, keys, values)


def local(queries, key_vectors, value_vectors, query_taps, key_taps, out_weight, doc_blocks):
    bf16 = jnp.bfloat16
    dma = pltpu.SemaphoreType.DMA
    shape = jax.ShapeDtypeStruct
    model = out_weight.shape[1]
    qx, gk, gv, w_share = pl.pallas_call(
        gather_kernel,
        out_shape=(
            shape((NX, NY, PIECE, QW), bf16),
            shape((NX, NY, NZ, NC, ROWS, HD), bf16),
            shape((NX, NY, NZ, NC, HD, ROWS), bf16),
            shape((NY, W_PIECES * W_PIECE, model // 2), bf16),
        ),
        in_specs=[ANY] * 6,
        out_specs=[ANY] * 4,
        scratch_shapes=[
            pltpu.VMEM((ROWS, 2 * QW), bf16),
            pltpu.VMEM((ROWS, 2 * HD), bf16),
            pltpu.VMEM((ROWS, 2 * HD), bf16),
            pltpu.VMEM((4, 2 * QW), jnp.float32),
            pltpu.VMEM((4, 2 * HD), jnp.float32),
            pltpu.VMEM((16, 2 * QW), bf16),
            pltpu.VMEM((16, 2 * HD), bf16),
            pltpu.VMEM((ROWS, 2 * QW), bf16),
            pltpu.VMEM((ROWS, 2 * HD), bf16),
            pltpu.VMEM((2 * HD, ROWS), bf16),
            dma((5,)), dma((2,)), dma((2,)), dma((2,)), dma((2,)), dma((2,)),
            dma((7,)), dma((7,)), dma, dma((2, W_PIECES + 1)), dma((2, W_PIECES + 1)),
            dma((4, 36)), dma((4, 36)),
        ],
        compiler_params=pltpu.CompilerParams(
            collective_id=0, has_side_effects=True, vmem_limit_bytes=60 << 20
        ),
        name="gather",
    )(queries, key_vectors, value_vectors, query_taps, key_taps, out_weight)

    attended = attend(
        doc_blocks,
        qx.reshape(NX * NY, PIECE, QW),
        gk.reshape(SEQ, HD),
        gv.reshape(SEQ // ROWS, HD, ROWS),
    )

    return pl.pallas_call(
        project_kernel,
        out_shape=shape((ROWS, model // 2), bf16),
        in_specs=[ANY] * 3,
        out_specs=VMEM,
        scratch_shapes=[
            pltpu.VMEM((4, ROWS, QW), bf16),
            pltpu.VMEM((ROWS, QW), bf16),
            pltpu.VMEM((2 * QW, model // 2), bf16),
            pltpu.VMEM((2 * QW, model // 2), bf16),
            pltpu.VMEM((model // 2 // TILE, ROWS, TILE), jnp.float32),
            dma((3, 2)), dma((3, 2)), dma((2,)), dma((3, 4)), dma((3, 4)),
            dma, dma((2,)), dma((14,)), dma((14,)),
        ],
        compiler_params=pltpu.CompilerParams(
            collective_id=1, has_side_effects=True, vmem_limit_bytes=48 << 20
        ),
        name="project",
    )(attended, out_weight, w_share)


def solution(mesh):
    in_specs = (
        P(("inner", "outer"), "head"),
        P(("inner", "outer"), "head"),
        P(("inner", "outer"), "head"),
        P(None, "head"),
        P(None, "head"),
        P("head", None),
        P(),
    )
    out_specs = P(("inner", "outer"), "head")
    return jax.shard_map(local, mesh=mesh, in_specs=in_specs, out_specs=out_specs, check_vma=False)
```

```python
import functools

import jax
import jax.numpy as jnp
from jax import lax
from jax.experimental import pallas as pl
from jax.experimental.pallas import tpu as pltpu
from jax.sharding import PartitionSpec as P

HD = 128
BLOCK = 128
NX, NY, NZ, NC = 4, 2, 4, 2
ROWS = 256
SEQ = 16384
GROUP = 6
PIECE = ROWS // NX
W_PIECES, W_PIECE = 6, 32
QW = GROUP * HD
CHUNK = 1024
LIMIT = 2.0**60
SPARE = 24
MESH = pl.DeviceIdType.MESH
VMEM = pl.BlockSpec(memory_space=pltpu.VMEM)
ANY = pl.BlockSpec(memory_space=pl.ANY)


def place():
    x = lax.axis_index("inner")
    outer = lax.axis_index("outer")
    return x, outer // (NZ * NC), (outer // NC) % NZ, outer % NC


def at(x, y, z, c):
    return {"inner": x, "outer": y * (NZ * NC) + z * NC + c}


def turn(i, n, d):
    return (i + n + d) % n


def far_rows(x, y, z, c, start, size):
    quarter = (x + z) % 2 + 2 * y
    return pl.ds(pl.multiple_of(quarter * 384 + c * 192 + start, 16), size)


def greet(others):
    barrier = pltpu.get_barrier_semaphore()
    for other in others:
        pl.semaphore_signal(barrier, inc=1, device_id=other, device_id_type=MESH)
    pl.semaphore_wait(barrier, len(others))


def remote(src, dst, send, recv, to):
    return pltpu.make_async_remote_copy(
        src_ref=src, dst_ref=dst, send_sem=send, recv_sem=recv, device_id=to, device_id_type=MESH
    )


def convolve(halo, field, taps, out, width, tile):
    def one(i, carry):
        cols = pl.ds(pl.multiple_of(i * tile, tile), tile)
        wide = jnp.concatenate(
            [halo[:, cols].astype(jnp.float32), field[:, cols].astype(jnp.float32)], axis=0
        )
        total = taps[0:1, cols] * wide[16:]
        for j in range(1, 4):
            total = total + taps[j : j + 1, cols] * wide[16 - j : 16 - j + ROWS]
        out[:, cols] = total.astype(jnp.bfloat16)
        return carry

    lax.fori_loop(0, width // tile, one, 0)


def gather_kernel(
    q_hbm, k_hbm, v_hbm, qt_hbm, kt_hbm, w_hbm, qx_ref, gk_ref, gv_ref, w_ref,
    q_ref, k_ref, v_ref, qt_ref, kt_ref,
    halo_q, halo_k, cq, ck, vt, load_s, halo_s, halo_r, y_s, y_r, own_s, q_s, q_r, q_own, w_s, w_r, send, recv,
):
    x, y, z, c = place()
    head = lax.axis_index("head")
    loads = [
        pltpu.make_async_copy(src, dst, load_s.at[i])
        for i, (src, dst) in enumerate(
            ((k_hbm, k_ref), (v_hbm, v_ref), (kt_hbm, kt_ref), (q_hbm, q_ref), (qt_hbm, qt_ref))
        )
    ]
    for load in loads:
        load.start()
    shard = x * 16 + lax.axis_index("outer")
    after = turn(shard, 64, 1)
    before = turn(shard, 64, -1)
    nxt = {"inner": after // 16, "outer": after % 16}
    prv = {"inner": before // 16, "outer": before % 16}
    across = at(x, 1 - y, z, c)
    opposite = {"head": 1 - head, **across}
    sibling = at(x, y, z, 1 - c)
    steps = {
        "z": (at(x, y, turn(z, NZ, 1), c), at(x, y, turn(z, NZ, -1), c)),
        "x": (at(turn(x, NX, 1), y, z, c), at(turn(x, NX, -1), y, z, c)),
    }
    peers = [
        (dx, dy) for dx in (0, 1, -1, 2) for dy in (0, 1) if (dx, dy) != (0, 0)
    ]
    peer_ids = [at(turn(x, NX, dx), (y + dy) % 2, z, c) for dx, dy in peers]
    greet(
        [nxt, prv, across, opposite, sibling, *steps["z"], *steps["x"]]
        + [d for d, (dx, dy) in zip(peer_ids, peers) if dx == 2 or dy == 1 and dx != 0]
    )

    halos = [
        remote(k_hbm.at[pl.ds(ROWS - 16, 16)], halo_k, halo_s.at[0], halo_r.at[0], nxt),
        remote(q_hbm.at[pl.ds(ROWS - 16, 16)], halo_q, halo_s.at[1], halo_r.at[1], nxt),
    ]
    for copy in halos:
        copy.start()

    mine = pl.ds(pl.multiple_of(y * HD, HD), HD)
    theirs = pl.ds(pl.multiple_of((1 - y) * HD, HD), HD)

    class Part:
        pass

    parts = []
    for index, (full, size, block_y, first, second) in enumerate((
        (gv_ref, HD, y, "x", "z"),
        (gk_ref, ROWS, y, "z", "x"),
        (gv_ref, HD, 1 - y, "x", "z"),
        (gk_ref, ROWS, 1 - y, "z", "x"),
    )):
        part = Part()
        part.index, part.full, part.size, part.y = index, full, size, block_y
        part.first, part.second = steps[first], steps[second]
        part.swap = first == "x"
        part.sends = []
        parts.append(part)
    v_mine, k_mine, v_theirs, k_theirs = parts

    def block(part, da, db, half=None, core=c):
        xx, zz = (turn(x, NX, da), turn(z, NZ, db)) if part.swap else (turn(x, NX, db), turn(z, NZ, da))
        rows = pl.ds(0, part.size) if half is None else pl.ds(half * part.size // 2, part.size // 2)
        return part.full.at[xx, part.y, zz, core, rows]

    def push(part, ref, to, slot, src=None):
        copy = remote(ref if src is None else src, ref, send.at[part.index, slot], recv.at[part.index, slot], to)
        copy.start()
        part.sends.append(copy)

    def landed(part, ref, slot):
        remote(ref, ref, send.at[part.index, slot], recv.at[part.index, slot], across).wait_recv()

    offsets = (0, -1, 1, 2)
    def to_sibling(part, da, db, src=None):
        push(part, block(part, da, db), sibling, 20 + offsets.index(da) * 4 + offsets.index(db), src)

    def second_ring(part, da, src=None):
        k = offsets.index(da)
        for side in range(2):
            push(part, block(part, da, 0), part.second[side], 4 + 2 * k + side, src)
        to_sibling(part, da, 0, src)

    def begin(part, src=None):
        for side in range(2):
            push(part, block(part, 0, 0), part.first[side], side, src)
        second_ring(part, 0, src)

    def ring_step(part):
        landed(part, block(part, -1, 0), 0)
        push(part, block(part, -1, 0, 0), part.first[0], 2)
        landed(part, block(part, 1, 0), 1)
        push(part, block(part, 1, 0, 1), part.first[1], 3)
        second_ring(part, -1)
        second_ring(part, 1)

    def ring_end(part):
        landed(part, block(part, 2, 0, 0), 2)
        landed(part, block(part, 2, 0, 1), 3)
        second_ring(part, 2)

    def pass_on(part, da):
        k = offsets.index(da)
        landed(part, block(part, da, -1), 4 + 2 * k)
        push(part, block(part, da, -1, 0), part.second[0], 12 + 2 * k)
        landed(part, block(part, da, 1), 5 + 2 * k)
        push(part, block(part, da, 1, 1), part.second[1], 13 + 2 * k)
        to_sibling(part, da, -1)
        to_sibling(part, da, 1)

    def finish(part, da):
        k = offsets.index(da)
        landed(part, block(part, da, 2, 0), 12 + 2 * k)
        landed(part, block(part, da, 2, 1), 13 + 2 * k)
        to_sibling(part, da, 2)

    def to_across(part, src):
        copy = remote(src, part.full.at[x, y, z, c], y_s.at[part.index], y_r.at[part.index], across)
        copy.start()
        part.sends.append(copy)

    def from_across(part, source):
        ref = block(part, 0, 0)
        remote(ref, ref, y_s.at[source.index], y_r.at[source.index], across).wait_recv()

    def keep(part, src):
        part.own = pltpu.make_async_copy(src, block(part, 0, 0), own_s.at[part.index])
        part.own.start()

    loads[1].wait()
    vt[...] = v_ref[...].T
    to_across(v_mine, vt.at[theirs])
    begin(v_mine, vt.at[mine])
    keep(v_mine, vt.at[mine])

    loads[0].wait()
    loads[2].wait()
    halos[0].wait_recv()

    @pl.when(shard == 0)
    def _():
        halo_k[...] = jnp.zeros_like(halo_k)

    convolve(halo_k, k_ref, kt_ref, ck, 2 * HD, 128)
    to_across(k_mine, ck.at[:, theirs])
    begin(k_mine, ck.at[:, mine])
    keep(k_mine, ck.at[:, mine])

    half = w_hbm.shape[1] // 2
    w_columns = pl.ds(pl.multiple_of((1 - head) * half, half), half)

    def w_copy(k, origin, to, stage, slot=None):
        dst = w_ref.at[origin, pl.ds(k * W_PIECE, W_PIECE)]
        src = dst if stage else w_hbm.at[far_rows(x, origin, z, c, k * W_PIECE, W_PIECE), w_columns]
        slot = k if slot is None else slot
        return remote(src, dst, w_s.at[stage, slot], w_r.at[stage, slot], to)

    def w_fetches(origin):
        for k in range(W_PIECES):
            yield w_copy(k, origin, opposite, 0)
        yield w_copy(W_PIECES - 1, 1 - origin, opposite, 0, W_PIECES)

    for copy in w_fetches(1 - y):
        copy.start()

    def w_onward(k):
        w_copy(k, y, across, 0).wait_recv()
        w_copy(k, y, across, 1).start()

    from_across(v_theirs, v_mine)
    begin(v_theirs)
    ring_step(v_mine)
    from_across(k_theirs, k_mine)
    begin(k_theirs)
    ring_step(k_mine)

    ring_end(v_mine)
    ring_step(v_theirs)
    w_onward(0)
    loads[3].wait()
    loads[4].wait()
    halos[1].wait_recv()

    @pl.when(shard == 0)
    def _():
        halo_q[...] = jnp.zeros_like(halo_q)

    convolve(halo_q, q_ref, qt_ref, cq, 2 * QW, 128)

    q_copies = []
    for i, ((dx, dy), to) in enumerate(zip(peers, peer_ids)):
        px, py = turn(x, NX, dx), (y + dy) % 2
        piece = cq.at[
            pl.ds(pl.multiple_of(px * PIECE, PIECE), PIECE), pl.ds(pl.multiple_of(py * QW, QW), QW)
        ]
        copy = remote(piece, qx_ref.at[x, y], q_s.at[i], q_r.at[i], to)
        copy.start()
        q_copies.append(copy)
    own_q = pltpu.make_async_copy(
        cq.at[
            pl.ds(pl.multiple_of(x * PIECE, PIECE), PIECE), pl.ds(pl.multiple_of(y * QW, QW), QW)
        ],
        qx_ref.at[x, y],
        q_own,
    )
    own_q.start()

    ring_end(k_mine)
    ring_step(k_theirs)
    ring_end(v_theirs)
    ring_end(k_theirs)
    w_onward(1)
    for i, da in enumerate(offsets):
        for part in parts:
            pass_on(part, da)
        if i % 2:
            w_onward(2 + i // 2)
    for i, da in enumerate(offsets):
        for part in parts:
            finish(part, da)
        if i == 1:
            w_onward(4)

    for part in parts:
        for copy in part.sends:
            copy.wait_send()
        for i, da in enumerate(offsets):
            for j, db in enumerate(offsets):
                landed(part, block(part, da, db, core=1 - c), 20 + 4 * i + j)
    v_mine.own.wait()
    k_mine.own.wait()
    for copy in halos:
        copy.wait_send()
    for i, (dx, dy) in enumerate(peers):
        q_copies[i].wait_send()
        ref = qx_ref.at[turn(x, NX, -dx), (y + dy) % 2]
        remote(ref, ref, q_s.at[i], q_r.at[i], across).wait_recv()
    own_q.wait()
    for copy in w_fetches(1 - y):
        copy.wait_send()
    w_copy(W_PIECES - 1, y, opposite, 0).wait_recv()
    w_copy(W_PIECES - 1, 1 - y, opposite, 0, W_PIECES).wait_recv()
    for k in range(W_PIECES - 1):
        w_copy(k, y, across, 1).wait_send()
        w_copy(k, 1 - y, across, 1).wait_recv()


def find_spans(doc_ref, first_ref, limit_ref):
    x = lax.axis_index("inner")
    outer = lax.axis_index("outer")
    for p in range(NX * NY):
        token = ((p // NY) * 16 + (p % NY) * 8 + outer % 8) * ROWS + x * PIECE
        start = jnp.int32(0)
        first = jnp.int32(0)
        for d in range(doc_ref.shape[0]):
            first = jnp.where(start <= token, start, first)
            start = start + doc_ref[d] * BLOCK
        first_ref[p] = first
        limit_ref[p] = token + PIECE


def attend_kernel(doc_ref, q_ref, gk_ref, gv_ref, o_ref, first_ref, limit_ref, keys, values, q_all, o_all, q_t, acc, add, l_s, l_n, m_s, q_sem, o_sem, k_sem, v_sem):
    def key_load(i):
        rows = pl.ds(pl.multiple_of(i * CHUNK, CHUNK), CHUNK)
        return pltpu.make_async_copy(gk_ref.at[rows], keys.at[rows], k_sem.at[i])

    def value_load(i):
        columns = pl.ds(pl.multiple_of(i * ROWS, ROWS), ROWS)
        return pltpu.make_async_copy(gv_ref.at[i], values.at[:, columns], v_sem.at[i])

    def start_loads(i, carry):
        key_load(i).start()
        for u in range(CHUNK // ROWS):
            value_load(i * (CHUNK // ROWS) + u).start()
        return carry

    q_load = pltpu.make_async_copy(q_ref, q_all, q_sem)
    q_load.start()
    lax.fori_loop(0, SEQ // CHUNK, start_loads, 0)
    find_spans(doc_ref, first_ref, limit_ref)
    keys[SEQ:, :] = jnp.zeros((ROWS, HD), jnp.bfloat16)
    values[:, SEQ:] = jnp.zeros((HD, ROWS), jnp.bfloat16)
    q_load.wait()
    for p in range(NX * NY):
        for h in range(GROUP):
            q_t[p, :, h * PIECE : (h + 1) * PIECE] = q_all[p, :, h * HD : (h + 1) * HD].T

    def wait_loads(i, carry):
        key_load(i).wait()
        for u in range(CHUNK // ROWS):
            value_load(i * (CHUNK // ROWS) + u).wait()
        return carry

    factor = HD**-0.5 * 1.4426950408889634
    width = GROUP * PIECE

    def store(p):
        return pltpu.make_async_copy(o_all.at[p], o_ref.at[p], o_sem.at[p])

    def position(p, carry):
        @pl.when(p % NY == 0)
        def _():
            loads = SEQ // CHUNK // NX
            lax.fori_loop(p // NY * loads, (p // NY + 1) * loads, wait_loads, 0)

        first = first_ref[p]
        limit = limit_ref[p]
        pieces = (limit - first + ROWS - 1) // ROWS
        count = (pieces - 1) // (CHUNK // ROWS)
        rest = pieces - count * (CHUNK // ROWS)

        def scores(start, size):
            return jnp.dot(keys[pl.ds(start, size), :], q_t[p], preferred_element_type=jnp.float32)

        def mix(start, size, weights):
            return jnp.dot(values[:, pl.ds(start, size)], weights, preferred_element_type=jnp.float32)

        def add_up(exps, size):
            return jnp.sum(exps.reshape(size // 8, 8, width), axis=0)

        def tail(size):
            start = pl.multiple_of(first + count * CHUNK, BLOCK)
            s = scores(start, size)
            token = limit - PIECE + lax.rem(
                lax.broadcasted_iota(jnp.int32, (ROWS, width), 1), PIECE
            )
            key = start + size - ROWS + lax.broadcasted_iota(jnp.int32, (ROWS, width), 0)
            edge = jnp.where(key <= token, s[size - ROWS :], -1e30)
            s = edge if size == ROWS else jnp.concatenate([s[: size - ROWS], edge], axis=0)
            top = jnp.max(s, axis=0, keepdims=True)
            exps = jnp.exp2((s - top) * factor)
            l_s[...] = add_up(exps, size)
            m_s[...] = jnp.broadcast_to(top, m_s.shape)
            acc[...] = mix(start, size, exps.astype(jnp.bfloat16))

        for k in range(1, CHUNK // ROWS + 1):
            pl.when(rest == k)(functools.partial(tail, k * ROWS))

        def chunk(start, size):
            exps = jnp.exp2((scores(start, size) - m_s[0:1, :]) * factor)
            totals = l_s[...] + add_up(exps, size)
            add[...] = mix(start, size, exps.astype(jnp.bfloat16))
            l_n[...] = totals
            high = jnp.logical_not(jnp.max(totals) <= LIMIT)

            @pl.when(jnp.logical_not(high))
            def _():
                acc[...] = acc[...] + add[...]
                l_s[...] = l_n[...]

            @pl.when(high)
            def _():
                def redo(i, carry):
                    at_rows = pl.multiple_of(start + i * CHUNK, BLOCK)
                    s = scores(at_rows, CHUNK)
                    old = m_s[0:1, :]
                    top = jnp.maximum(old, jnp.max(s, axis=0, keepdims=True))
                    decay = jnp.exp2((old - top) * factor)
                    exps = jnp.exp2((s - top) * factor)
                    l_s[...] = l_s[...] * decay + add_up(exps, CHUNK)
                    m_s[...] = jnp.broadcast_to(top, m_s.shape)
                    acc[...] = acc[...] * decay + mix(at_rows, CHUNK, exps.astype(jnp.bfloat16))
                    return carry

                lax.fori_loop(0, size // CHUNK, redo, 0)

        def long_chunk(i, carry):
            chunk(pl.multiple_of(first + i * 3 * CHUNK, BLOCK), 3 * CHUNK)
            return carry

        lax.fori_loop(0, count // 3, long_chunk, 0)
        rest_at = pl.multiple_of(first + count // 3 * 3 * CHUNK, BLOCK)
        for k in (1, 2):
            pl.when(count % 3 == k)(functools.partial(chunk, rest_at, k * CHUNK))

        totals = jnp.sum(l_s[...], axis=0, keepdims=True)
        result = (acc[...] / totals).T
        for h in range(GROUP):
            o_all[p, :, h * HD : (h + 1) * HD] = result[h * PIECE : (h + 1) * PIECE].astype(
                jnp.bfloat16
            )
        store(p).start()
        return carry

    lax.fori_loop(0, NX * NY, position, 0)
    for p in range(NX * NY):
        store(p).wait()


TILE = 512


def project_kernel(
    o_ref, w_ref, share_ref, out_ref, full, other, w_own, w_far, total,
    x_s, x_r, o_s, y_s, y_r, w_s, own_s, send, recv,
):
    x, y, z, c = place()
    head = lax.axis_index("head")
    group = 2 * head + y
    half = w_ref.shape[1] // 2
    tiles = half // TILE
    sibling = at(x, y, z, 1 - c)
    z_ids = [at(x, y, turn(z, NZ, d), c) for d in (1, -1)]
    x_ids = [at(turn(x, NX, d), y, z, c) for d in (1, -1, 2)]
    across = at(x, 1 - y, z, c)
    y_ids = [across, {"head": 1 - head, **across}, {"head": 1 - head, **at(x, y, z, c)}]

    w_load = pltpu.make_async_copy(
        w_ref.at[:, pl.ds(pl.multiple_of(head * half, half), half)], w_own, w_s
    )
    greet([sibling, *z_ids, *x_ids, *y_ids])

    def piece(xx):
        return pl.ds(pl.multiple_of(xx * PIECE, PIECE), PIECE)

    here = piece(x)
    x_copies = []
    for i, (d, to) in enumerate(zip((1, -1, 2), x_ids)):
        xx = turn(x, NX, d)
        for j, copy in enumerate((
            remote(o_ref.at[xx * NY + 1 - y], other.at[here], x_s.at[i, 0], x_r.at[i, 0], to),
            remote(o_ref.at[xx * NY + y], full.at[group, here], x_s.at[i, 1], x_r.at[i, 1], to),
        )):
            copy.start()
            x_copies.append(copy)
    own_copies = [
        pltpu.make_async_copy(o_ref.at[x * NY + 1 - y], other.at[here], o_s.at[0]),
        pltpu.make_async_copy(o_ref.at[x * NY + y], full.at[group, here], o_s.at[1]),
    ]
    for copy in own_copies:
        copy.start()

    sent = []

    def push(src, dst, slot, to):
        copy = remote(src, dst, send.at[slot], recv.at[slot], to)
        copy.start()
        sent.append(copy)

    def landed(ref, slot):
        remote(ref, ref, send.at[slot], recv.at[slot], sibling).wait_recv()

    for j in range(2):
        for k in range(2):
            rows = far_rows(x, j, z, c, 64 * k, 64)
            push(share_ref.at[j, pl.ds(64 * k, 64)], w_far.at[rows], 2 * j + k, z_ids[j])
        rows = far_rows(x, j, z, c, 128, 64)
        push(share_ref.at[j, pl.ds(128, 64)], w_far.at[rows], 4 + j, x_ids[j])
    own_shares = []
    for j in range(2):
        mine = w_far.at[far_rows(x, j, z, c, 0, 192)]
        push(share_ref.at[j], mine, 6 + j, sibling)
        own_shares.append(pltpu.make_async_copy(share_ref.at[j], mine, own_s.at[j]))
        own_shares[j].start()
    w_load.start()

    y_copies = []

    def onward(i, xx):
        rows = piece(xx)
        for r, (src, to) in enumerate(
            zip((other.at[rows], other.at[rows], full.at[group, rows]), y_ids)
        ):
            copy = remote(src, full.at[group, rows], y_s.at[r, i], y_r.at[r, i], to)
            copy.start()
            y_copies.append(copy)

    for copy in own_copies:
        copy.wait()
    onward(3, x)
    for i, d in enumerate((1, -1, 2)):
        xx = turn(x, NX, -d)
        rows = piece(xx)
        remote(other.at[rows], other.at[rows], x_s.at[i, 0], x_r.at[i, 0], sibling).wait_recv()
        ref = full.at[group, rows]
        remote(ref, ref, x_s.at[i, 1], x_r.at[i, 1], sibling).wait_recv()
        onward(i, xx)

    def multiply(g, column, depth, w, row, first=False, last=False):
        def one(t, carry):
            cols = pl.ds(pl.multiple_of(t * TILE, TILE), TILE)
            value = jnp.dot(
                full[g, :, pl.ds(column, depth)], w[pl.ds(row, depth), cols], preferred_element_type=jnp.float32
            )
            if not first:
                value = value + total[t]
            if last:
                out_ref[:, cols] = value.astype(jnp.bfloat16)
            else:
                total[t] = value
            return carry

        lax.fori_loop(0, tiles, one, 0)

    w_load.wait()
    multiply(group, 0, QW, w_own, pl.multiple_of(y * QW, QW), first=True)

    def await_group(r, g):
        for i, d in enumerate((1, -1, 2, 0)):
            ref = full.at[g, piece(turn(x, NX, -d))]
            remote(ref, ref, y_s.at[r, i], y_r.at[r, i], sibling).wait_recv()

    await_group(0, group + 1 - 2 * y)
    multiply(group + 1 - 2 * y, 0, QW, w_own, pl.multiple_of((1 - y) * QW, QW))

    def arrivals(core):
        for j, d in enumerate((-1, 1)):
            yield 4 + j, 12 + j, w_far.at[far_rows(turn(x, NX, d), j, z, core, 128, 64)]
        for k in range(2):
            for j, d in enumerate((-1, 1)):
                yield 2 * j + k, 8 + 2 * j + k, w_far.at[far_rows(x, j, turn(z, NZ, d), core, 64 * k, 64)]

    for slot, onto, ref in arrivals(c):
        landed(ref, slot)
        push(ref, ref, onto, sibling)

    await_group(1, 3 - group)
    await_group(2, (group + 2) % 4)

    def far(parity, j, last=False):
        quarter = parity + 2 * j
        multiply(
            2 * (1 - head) + j,
            pl.multiple_of(parity * 384, 128),
            384,
            w_far,
            pl.multiple_of(quarter * 384, 384),
            last=last,
        )

    parity = (x + z) % 2
    for j in range(2):
        own_shares[j].wait()
        landed(w_far.at[far_rows(x, j, z, 1 - c, 0, 192)], 6 + j)
        far(parity, j)
    for slot, onto, ref in arrivals(1 - c):
        landed(ref, onto)
    for j in range(2):
        far(1 - parity, j, last=j == 1)

    for copy in (*x_copies, *sent, *y_copies):
        copy.wait_send()


def attend(doc_blocks, queries, keys, values):
    f32, bf16 = jnp.float32, jnp.bfloat16
    smem = pl.BlockSpec(memory_space=pltpu.SMEM)
    width = GROUP * PIECE
    return pl.pallas_call(
        attend_kernel,
        out_shape=jax.ShapeDtypeStruct((SPARE * NX * NY, PIECE, QW), bf16),
        in_specs=[smem, ANY, ANY, ANY],
        out_specs=ANY,
        scratch_shapes=[
            pltpu.SMEM((NX * NY,), jnp.int32),
            pltpu.SMEM((NX * NY,), jnp.int32),
            pltpu.VMEM((SEQ + ROWS, HD), bf16),
            pltpu.VMEM((HD, SEQ + ROWS), bf16),
            pltpu.VMEM((NX * NY, PIECE, QW), bf16),
            pltpu.VMEM((NX * NY, PIECE, QW), bf16),
            pltpu.VMEM((NX * NY, HD, width), bf16),
            pltpu.VMEM((HD, width), f32),
            pltpu.VMEM((HD, width), f32),
            pltpu.VMEM((8, width), f32),
            pltpu.VMEM((8, width), f32),
            pltpu.VMEM((8, width), f32),
            pltpu.SemaphoreType.DMA,
            pltpu.SemaphoreType.DMA((NX * NY,)),
            pltpu.SemaphoreType.DMA((SEQ // CHUNK,)),
            pltpu.SemaphoreType.DMA((SEQ // ROWS,)),
        ],
        compiler_params=pltpu.CompilerParams(vmem_limit_bytes=60 << 20),
        name="attend",
    )(doc_blocks, queries, keys, values)


def local(queries, key_vectors, value_vectors, query_taps, key_taps, out_weight, doc_blocks):
    bf16 = jnp.bfloat16
    dma = pltpu.SemaphoreType.DMA
    shape = jax.ShapeDtypeStruct
    model = out_weight.shape[1]
    qx, gk, gv, w_share = pl.pallas_call(
        gather_kernel,
        out_shape=(
            shape((NX, NY, PIECE, QW), bf16),
            shape((NX, NY, NZ, NC, ROWS, HD), bf16),
            shape((NX, NY, NZ, NC, HD, ROWS), bf16),
            shape((NY, W_PIECES * W_PIECE, model // 2), bf16),
        ),
        in_specs=[ANY] * 6,
        out_specs=[ANY] * 4,
        scratch_shapes=[
            pltpu.VMEM((ROWS, 2 * QW), bf16),
            pltpu.VMEM((ROWS, 2 * HD), bf16),
            pltpu.VMEM((ROWS, 2 * HD), bf16),
            pltpu.VMEM((4, 2 * QW), jnp.float32),
            pltpu.VMEM((4, 2 * HD), jnp.float32),
            pltpu.VMEM((16, 2 * QW), bf16),
            pltpu.VMEM((16, 2 * HD), bf16),
            pltpu.VMEM((ROWS, 2 * QW), bf16),
            pltpu.VMEM((ROWS, 2 * HD), bf16),
            pltpu.VMEM((2 * HD, ROWS), bf16),
            dma((5,)), dma((2,)), dma((2,)), dma((2,)), dma((2,)), dma((2,)),
            dma((7,)), dma((7,)), dma, dma((2, W_PIECES + 1)), dma((2, W_PIECES + 1)),
            dma((4, 36)), dma((4, 36)),
        ],
        compiler_params=pltpu.CompilerParams(
            collective_id=0, has_side_effects=True, vmem_limit_bytes=60 << 20
        ),
        name="gather",
    )(queries, key_vectors, value_vectors, query_taps, key_taps, out_weight)

    attended = attend(
        doc_blocks,
        qx.reshape(NX * NY, PIECE, QW),
        gk.reshape(SEQ, HD),
        gv.reshape(SEQ // ROWS, HD, ROWS),
    )

    return pl.pallas_call(
        project_kernel,
        out_shape=shape((ROWS, model // 2), bf16),
        in_specs=[ANY] * 3,
        out_specs=VMEM,
        scratch_shapes=[
            pltpu.VMEM((4, ROWS, QW), bf16),
            pltpu.VMEM((ROWS, QW), bf16),
            pltpu.VMEM((2 * QW, model // 2), bf16),
            pltpu.VMEM((2 * QW, model // 2), bf16),
            pltpu.VMEM((model // 2 // TILE, ROWS, TILE), jnp.float32),
            dma((3, 2)), dma((3, 2)), dma((2,)), dma((3, 4)), dma((3, 4)),
            dma, dma((2,)), dma((14,)), dma((14,)),
        ],
        compiler_params=pltpu.CompilerParams(
            collective_id=1, has_side_effects=True, vmem_limit_bytes=48 << 20
        ),
        name="project",
    )(attended, out_weight, w_share)


def solution(mesh):
    in_specs = (
        P(("inner", "outer"), "head"),
        P(("inner", "outer"), "head"),
        P(("inner", "outer"), "head"),
        P(None, "head"),
        P(None, "head"),
        P("head", None),
        P(),
    )
    out_specs = P(("inner", "outer"), "head")
    return jax.shard_map(local, mesh=mesh, in_specs=in_specs, out_specs=out_specs, check_vma=False)
```
